256 devices in a mesh: row: 32 (over z, y_lo, core), col: 4 (over x), rep: 2 (over y_hi).
Axes of the slice: x: 4, y: 4 (y_hi: 2, y_lo: 2; y = y_hi * 2 + y_lo), z: 8, core: 2. Of those that a mesh axis runs over, the one named last changes fastest.
Arguments:
- tracers: bfloat16 [16, 8388608], P('col', ('row', 'rep')), may hold values from -6 to 6
- winds: float32 [2, 8388608], P(None, ('row', 'rep')), may hold values from -6 to 6
- tile_owner: int32 [65536], P(('row', 'rep')), may hold values from 0 to 65535, as said below
- departure: int32 [65536, 3], P(('row', 'rep')), may hold values from 0 to 65535, as said below
Outputs:
- advected: bfloat16 [16, 8388608], P('col', ('row', 'rep'))
The draws below stay inside these ranges and needn't reach their ends.
Inputs may be any that keep to these rules, and one draw needn't show every extreme that they name: `tile_owner`: A permutation of the blocks; the tiles of each device along row+rep (in that order, 1024 a device) name exactly 16 blocks of every such device. Each departure block lies within 256 blocks of its own block, counted cyclically over the 65536 blocks; that distance is reached.
All inputs are finite; a program needn't handle non-finite values.
Results may differ from the reference program's by a relative error of at most 0.0048.
Values may be sent and summed in bfloat16 or wider, within the bound.
A program may use at most 64 MiB of HBM per device.

```python
import jax
import jax.numpy as jnp
from jax import lax

NTR = 16
BP = 1024
PIECES = 64
NBLK = 65536
CELLS = 8388608


def draw_tile_owner(key, part):
    key = jax.random.fold_in(key, 11)
    per = BP // PIECES
    key_rot, key_slot, key_dest = jax.random.split(key, 3)
    rotation = jax.random.randint(key_rot, (PIECES,), 0, PIECES)
    slot_order = jax.vmap(lambda k: jax.random.permutation(k, BP))(jax.random.split(key_slot, PIECES))
    sources = jnp.arange(PIECES)[:, None]
    target = (slot_order % PIECES + rotation[:, None]) % PIECES
    local_first = sources * per + slot_order // PIECES
    dest_order = jax.vmap(lambda k: jax.random.permutation(k, BP))(jax.random.split(key_dest, PIECES))
    owner = target * BP + dest_order[target, local_first]
    return owner.reshape(NBLK).astype(jnp.int32)


def draw_departure(key, part):
    key = jax.random.fold_in(key, 23)
    reach = BP // 4
    offset = jax.random.randint(key, (NBLK, 3), -reach, reach + 1)
    rows = jnp.arange(NBLK)
    lead = jnp.where(rows % BP == 0, reach, jnp.where(rows % BP == 1, -reach, offset[:, 0]))
    offset = offset.at[:, 0].set(lead)
    return jnp.mod(rows[:, None] + offset, NBLK).astype(jnp.int32)


def block_levels(rng, extent, shards, least, largest):
    def one(dim, blocks):
        heights = jax.random.uniform(jax.random.fold_in(jax.random.fold_in(rng, 6), dim), (blocks,), jnp.float32, least / len(shards), largest / len(shards))
        return jnp.repeat(jnp.exp(heights), extent[dim] // blocks).reshape((-1,) + (1,) * (len(extent) - dim - 1))

    loudness = one(*shards[0])
    for cut in shards[1:]:
        loudness = loudness * one(*cut)
    return loudness


def gaussian(key, dims, spread, most, shards=(), dtype=jnp.bfloat16):
    drawn = jax.random.normal(key, dims, jnp.float32) * spread
    if len(shards) > 0:
        drawn = block_levels(key, dims, shards, -0.22, 0.18) * drawn
    return jnp.clip(drawn, min=-most, max=most).astype(dtype)


def setup_inputs(seed: int = 0) -> dict:
    key_of = jax.random.split(jax.random.key(seed), 5)
    tracers = gaussian(key_of[0], (NTR, CELLS), 1.0, 6.0, ((0, 4), (1, 64)))
    winds = gaussian(key_of[1], (2, CELLS), 1.0, 6.0, ((1, 64),), jnp.float32)
    tile_owner = draw_tile_owner(jax.random.fold_in(key_of[4], 71), 0)
    departure = draw_departure(jax.random.fold_in(key_of[4], 71), 0)
    return dict(tracers=tracers, winds=winds, tile_owner=tile_owner, departure=departure)


def lagrange(frac):
    first = -frac * (frac - 1.0) * (frac - 2.0) / 6.0
    second = (frac + 1.0) * (frac - 1.0) * (frac - 2.0) / 2.0
    third = -(frac + 1.0) * frac * (frac - 2.0) / 2.0
    fourth = (frac + 1.0) * frac * (frac - 1.0) / 6.0
    return jnp.stack([first, second, third, fourth])


def stencil(wind_rows):
    cell = jnp.arange(128)
    arrive_y = (cell // 16).astype(jnp.float32) + 8.0
    arrive_x = (cell % 16).astype(jnp.float32)
    pos_y = arrive_y - 6.0 * jnp.tanh(wind_rows[0])
    pos_x = arrive_x - 4.0 * jnp.tanh(wind_rows[1])
    floor_y = jnp.floor(pos_y)
    floor_x = jnp.floor(pos_x)
    return floor_y.astype(jnp.int32), lagrange(pos_y - floor_y), floor_x.astype(jnp.int32), lagrange(pos_x - floor_x)


def build_tiles(floor_y, factor_y, floor_x, factor_x):
    rows_y = jnp.arange(24).astype(jnp.int32)
    cols_x = jnp.arange(16).astype(jnp.int32)
    weight_y = jnp.zeros(floor_y.shape + (24,), jnp.float32)
    weight_x = jnp.zeros(floor_x.shape + (16,), jnp.float32)
    for step in range(4):
        weight_y = weight_y + jnp.where(rows_y == (floor_y + step - 1)[..., None], factor_y[step][..., None], 0.0)
        weight_x = weight_x + jnp.where(cols_x == jnp.mod(floor_x + step - 1, 16)[..., None], factor_x[step][..., None], 0.0)
    tiles = weight_y[..., :, None] * weight_x[..., None, :]
    return tiles.reshape(floor_y.shape + (384,)).astype(jnp.bfloat16)


def reference(tracers, winds, tile_owner, departure):
    total = tile_owner.shape[0]
    tiles = winds.reshape(2, total, 128)
    wind_rows = jnp.take(tiles, jnp.argsort(tile_owner).astype(jnp.int32), axis=1)
    floor_y, factor_y, floor_x, factor_x = stencil(wind_rows)
    q_blocks = tracers.reshape(NTR, total, 128)
    group = 32
    count = total // group

    def apply(args):
        group_y, group_fy, group_x, group_fx, group_dep = args
        weights = build_tiles(group_y, group_fy, group_x, group_fx).astype(jnp.float32)
        source = jnp.take(q_blocks, group_dep.reshape(-1), axis=1).reshape(NTR, group, 384).astype(jnp.float32)
        return jnp.einsum("gic,tgc->tgi", weights, source).astype(jnp.bfloat16)

    result = lax.map(apply, (floor_y.reshape(count, group, 128),
                             jnp.moveaxis(factor_y.reshape(4, count, group, 128), 1, 0),
                             floor_x.reshape(count, group, 128),
                             jnp.moveaxis(factor_x.reshape(4, count, group, 128), 1, 0),
                             departure.reshape(count, group, 3)))
    return jnp.transpose(result, (1, 0, 2, 3)).reshape(NTR, total * 128)
```

```python
import functools

import jax
import jax.numpy as jnp
from jax import lax
from jax.experimental import pallas as pl
from jax.experimental.pallas import tpu as pltpu
from jax.sharding import PartitionSpec as P

f32, i32, bf16 = jnp.float32, jnp.int32, jnp.bfloat16
AXES = ("row", "rep")
MESH = pl.DeviceIdType.MESH
ROWS = 17
UNIT = 4096
STEP = 64


def iota(shape, dim):
    return lax.broadcasted_iota(i32, shape, dim)


def pick(cond):
    return jnp.where(cond, 1.0, 0.0).astype(bf16)


def bytes_of(code):
    return (code >> 8).astype(f32).astype(bf16), (code & 255).astype(f32).astype(bf16)


def joined(parts):
    y = (parts[:, 0:128] * 256.0 + parts[:, 128:256]).astype(i32)
    x = (parts[:, 256:384] * 256.0 + parts[:, 384:512]).astype(i32)
    return (y << 16) | (x & 65535)


def place_of(piece):
    return {"row": piece // 2, "rep": piece % 2}


def exchange(
    winds, owner, tracers, words, low, high,
    parts, snd, rcv, where, counts, send_sem, recv_sem, halo_send, halo_recv,
):
    pieces = snd.shape[0]
    blocks = winds.shape[0] // 2
    edge = low.shape[0]
    me = lax.axis_index(AXES)
    after = lax.rem(me + 1, pieces)
    before = lax.rem(me + pieces - 1, pieces)

    barrier = pltpu.get_barrier_semaphore()

    def greet(i, _):
        to = lax.rem(me + i, pieces)
        pl.semaphore_signal(barrier, inc=1, device_id=place_of(to), device_id_type=MESH)
        return 0

    lax.fori_loop(1, pieces, greet, 0)

    def encode(i, _):
        base = i * 64
        y = jnp.concatenate([winds[pl.ds((base + 8 * j) * 2, 8, stride=2), :] for j in range(8)], 0)
        x = jnp.concatenate([winds[pl.ds((base + 8 * j) * 2 + 1, 8, stride=2), :] for j in range(8)], 0)
        cy = jnp.round(jnp.tanh(y) * (6.0 * UNIT)).astype(i32)
        cx = jnp.round(jnp.tanh(x) * (4.0 * UNIT)).astype(i32)
        parts[pl.ds(pl.multiple_of(base, 64), 64), :] = jnp.concatenate(bytes_of(cy) + bytes_of(cx), 1)
        return 0

    lax.fori_loop(0, blocks // 64, encode, 0)

    lanes = iota((128, 128), 1)
    step = jnp.concatenate([pick(iota((128, 128), 0) < lanes), jnp.ones((128, 128), bf16)], 1)
    run = jnp.zeros((pieces, 128), f32)
    sums = jnp.zeros((pieces, 128), f32)
    first_lane = lax.rem(me, 8) * 16
    for g in range(blocks // 128):
        own = owner[g : g + 1, :]
        to = own // blocks
        slot = own - to * blocks
        mine = iota((pieces, 128), 0) == to
        hot = pick(mine)
        seen = jnp.dot(hot, step, preferred_element_type=f32)
        rank = jnp.sum(jnp.where(mine, seen[:, :128] + run, 0.0), axis=0, keepdims=True)
        rank = rank.astype(i32)
        run = run + seen[:, 128:]
        where[g : g + 1, :] = to * 16 + rank
        here = iota((128, 128), 0) == rank + first_lane
        for part, scale in ((slot >> 5, 32.0), (slot & 31, 1.0)):
            spread = jnp.where(here, part.astype(f32), 0.0).astype(bf16)
            sums = sums + scale * lax.dot_general(
                hot, spread, (((1,), (1,)), ((), ())), preferred_element_type=f32
            )
    counts[...] = sums.astype(i32)

    def order(i, _):
        base = i * 128
        hot = jnp.concatenate(
            [pick(iota((128, 128), 0) + base == where[g : g + 1, :]) for g in range(blocks // 128)], 1
        )
        word = joined(jnp.dot(hot, parts[...], preferred_element_type=f32))
        for j in range(8):
            snd[i * 8 + j, 0:16, :] = word[16 * j : 16 * j + 16]
            snd[i * 8 + j, 16:17, :] = counts[pl.ds(i * 8 + j, 1), :]
        return 0

    lax.fori_loop(0, blocks // 128, order, 0)

    pl.semaphore_wait(barrier, pieces - 1)

    def message(to, frm):
        return pltpu.make_async_remote_copy(
            src_ref=snd.at[to, pl.ds(0, ROWS)],
            dst_ref=rcv.at[frm, pl.ds(0, ROWS)],
            send_sem=send_sem.at[to],
            recv_sem=recv_sem.at[frm],
            device_id=place_of(to),
            device_id_type=MESH,
        )

    def start(i, _):
        message(lax.rem(me + i, pieces), me).start()
        return 0

    lax.fori_loop(1, pieces, start, 0)

    up = pltpu.make_async_remote_copy(
        src_ref=tracers.at[pl.ds(tracers.shape[0] - edge, edge)],
        dst_ref=low,
        send_sem=halo_send.at[0],
        recv_sem=halo_recv.at[0],
        device_id=place_of(after),
        device_id_type=MESH,
    )
    down = pltpu.make_async_remote_copy(
        src_ref=tracers.at[pl.ds(0, edge)],
        dst_ref=high,
        send_sem=halo_send.at[1],
        recv_sem=halo_recv.at[1],
        device_id=place_of(before),
        device_id_type=MESH,
    )
    up.start()
    down.start()
    rcv[me, 0:24, :] = snd[me, 0:24, :]

    def finish(i, _):
        other = lax.rem(me + i, pieces)
        copy = message(other, other)
        copy.wait_send()
        copy.wait_recv()
        return 0

    lax.fori_loop(1, pieces, finish, 0)

    for g in range(blocks // 128):
        where[g : g + 1, :] = functools.reduce(
            jnp.add, [rcv[g * 8 + s, 16:17, :] for s in range(8)]
        )

    def unpack(i, _):
        word = rcv[pl.ds(i * 4, 4), 0:16, :].reshape(64, 128)
        y, x = word >> 16, (word << 16) >> 16
        parts[pl.ds(pl.multiple_of(i * 64, 64), 64), :] = jnp.concatenate(bytes_of(y) + bytes_of(x), 1)
        return 0

    lax.fori_loop(0, blocks // 64, unpack, 0)

    def settle(i, _):
        base = i * 128
        hot = jnp.concatenate(
            [pick(iota((128, 128), 0) + base == where[g : g + 1, :]) for g in range(blocks // 128)], 1
        )
        words[pl.ds(pl.multiple_of(base, 128), 128), :] = joined(
            jnp.dot(hot, parts[...], preferred_element_type=f32)
        )
        return 0

    lax.fori_loop(0, blocks // 128, settle, 0)
    up.wait()
    down.wait()


def lagrange(t):
    a, b, c = t + 1.0, t - 1.0, t - 2.0
    tb, ac = t * b, a * c
    return tb * c * (-1.0 / 6.0), ac * b * 0.5, ac * t * (-0.5), a * tb * (1.0 / 6.0)


def rows_at(x, index):
    return jnp.take_along_axis(x, index, axis=0, mode="promise_in_bounds")


def folded(a, b, d):
    sub = iota((8, 128), 0)
    mine = (sub & d) == 0
    kept, moved = jnp.where(mine, a, b), jnp.where(mine, b, a)
    return kept + rows_at(moved, sub ^ d)


def transport(dep, words, tracers, low, high, out, spread, fact_y, fact_x, floors):
    blocks = words.shape[0]
    reach = low.shape[0] // 4
    total = blocks * lax.axis_size(AXES)
    shift = reach - lax.axis_index(AXES) * blocks + total
    cell_row = iota((8, 128), 1) >> 4
    cell_col = iota((8, 128), 1) & 15
    sub = iota((8, 128), 0)
    zero = jnp.zeros((8, 128), f32)

    def widen(ref, first):
        def one(i, _):
            x = ref[pl.ds(pl.multiple_of(i * 32, 32), 32), :].astype(f32)
            own = cell_row == sub
            y = jnp.where(own[None], jnp.broadcast_to(x[:, None, :], (32, 8, 128)), 0.0)
            spread[pl.ds(pl.multiple_of((first + i) * 256, 256), 256), :] = y.reshape(256, 128).astype(bf16)
            return 0

        lax.fori_loop(0, ref.shape[0] // 32, one, 0)

    widen(low, 0)
    widen(tracers, reach // 8)
    widen(high, (reach + blocks) // 8)

    def clear(i, _):
        at = pl.ds(pl.multiple_of(i * 512, 512), 512)
        fact_y[at, :] = jnp.zeros((512, 128), f32)
        fact_x[at, :] = jnp.zeros((512, 128), f32)
        return 0

    lax.fori_loop(0, blocks // 64, clear, 0)

    def factors(i, _):
        for u in range(4):
            g = i * 4 + u
            at = pl.ds(pl.multiple_of(g * 8, 8), 8)
            word = words[at, :]
            pos_y = (cell_row + 8) * UNIT - (word >> 16)
            pos_x = cell_col * UNIT - ((word << 16) >> 16)
            wy = lagrange((pos_y & (UNIT - 1)).astype(f32) * (1.0 / UNIT))
            wx = lagrange((pos_x & (UNIT - 1)).astype(f32) * (1.0 / UNIT))
            for p in range(4):
                fact_y[pl.ds(g * 64 + p, 8, stride=8), :] = wy[p]
                fact_x[pl.ds(g * 64 + p, 8, stride=8), :] = wx[p]
            floors[0, at, :] = pos_y >> 12
            floors[1, at, :] = pos_x >> 12
        return 0

    lax.fori_loop(0, blocks // 32, factors, 0)

    def two_blocks(first):
        prods = []
        for e in (0, 1):
            b = first + e
            lines = []
            for k in range(3):
                d = (dep[k, b] + shift) & (total - 1)
                lines.append(spread[pl.ds(pl.multiple_of(d * 32, 32), 32), :])
            uy = (sub + 1) - jnp.broadcast_to(floors[0, pl.ds(b, 1), :], (8, 128))
            ux = (sub + 1) - jnp.broadcast_to(floors[1, pl.ds(b, 1), :], (8, 128))
            at = pl.ds(pl.multiple_of(b * 8, 8), 8)
            gy = rows_at(fact_y[at, :], uy & 7)
            gx = rows_at(fact_x[at, :], ux & 7)
            near = (ux & 8) == 0
            cols = jnp.concatenate([jnp.where(near, gx, zero), jnp.where(near, zero, gx)], 0).astype(bf16)
            sums = jnp.dot(
                jnp.concatenate(lines, 0), jnp.concatenate([cols] * 8, 0), preferred_element_type=f32
            )
            in0, in1 = uy >= 0, uy >= -8
            for t in range(4):
                r0, r1, r2 = (sums[32 * k + 8 * t : 32 * k + 8 * t + 8] for k in range(3))
                prods.append(jnp.where(in0, r0, jnp.where(in1, r1, r2)) * gy)
        for d in (4, 2, 1):
            prods = [folded(prods[i], prods[i + d], d) for i in range(d)]
        return prods[0]

    def some(i, _):
        for q in range(0, STEP, 4):
            b = i * STEP + q
            four = jnp.concatenate([two_blocks(b), two_blocks(b + 2)], 0).astype(bf16)
            out[pl.ds(pl.multiple_of(b * 4, 16), 16), :] = four
        return 0

    lax.fori_loop(0, blocks // STEP, some, 0)


def in_vmem(n):
    return [pl.BlockSpec(memory_space=pltpu.VMEM)] * n


def on_device(tracers, winds, tile_owner, departure):
    pieces = lax.axis_size(AXES)
    blocks = tile_owner.shape[0]
    panel = tracers.shape[0]
    edge = blocks // 4 * panel
    lines = tracers.reshape(panel, blocks, 128).transpose(1, 0, 2).reshape(blocks * panel, 128)
    wind_lines = winds.reshape(2, blocks, 128).transpose(1, 0, 2).reshape(blocks * 2, 128)
    words, low, high = pl.pallas_call(
        exchange,
        out_shape=(
            jax.ShapeDtypeStruct((blocks, 128), i32),
            jax.ShapeDtypeStruct((edge, 128), bf16),
            jax.ShapeDtypeStruct((edge, 128), bf16),
        ),
        in_specs=in_vmem(3),
        out_specs=tuple(in_vmem(3)),
        scratch_shapes=[
            pltpu.VMEM((blocks, 512), bf16),
            pltpu.VMEM((pieces, 24, 128), i32),
            pltpu.VMEM((pieces, 24, 128), i32),
            pltpu.VMEM((8, 128), i32),
            pltpu.VMEM((pieces, 128), i32),
            pltpu.SemaphoreType.DMA((pieces,)),
            pltpu.SemaphoreType.DMA((pieces,)),
            pltpu.SemaphoreType.DMA((2,)),
            pltpu.SemaphoreType.DMA((2,)),
        ],
        compiler_params=pltpu.CompilerParams(
            collective_id=0, has_side_effects=True, vmem_limit_bytes=40 << 20
        ),
    )(wind_lines, tile_owner.reshape(blocks // 128, 128), lines)
    out = pl.pallas_call(
        transport,
        out_shape=jax.ShapeDtypeStruct((blocks * panel, 128), bf16),
        in_specs=[pl.BlockSpec(memory_space=pltpu.SMEM)] + in_vmem(4),
        out_specs=in_vmem(1)[0],
        scratch_shapes=[
            pltpu.VMEM((blocks * 48, 128), bf16),
            pltpu.VMEM((blocks * 8, 128), f32),
            pltpu.VMEM((blocks * 8, 128), f32),
            pltpu.VMEM((2, blocks, 128), i32),
        ],
        compiler_params=pltpu.CompilerParams(vmem_limit_bytes=48 << 20),
    )(departure.T, words, lines, low, high)
    return out.reshape(blocks, panel, 128).transpose(1, 0, 2).reshape(panel, blocks * 128)


def solution(mesh):
    placed = (
        P("col", AXES),
        P(None, AXES),
        P(AXES),
        P(AXES, None),
    )
    return jax.shard_map(
        on_device, mesh=mesh, in_specs=placed, out_specs=P("col", AXES), check_vma=False
    )
```

```python
import functools

import jax
import jax.numpy as jnp
from jax import lax
from jax.experimental import pallas as pl
from jax.experimental.pallas import tpu as pltpu
from jax.sharding import PartitionSpec as P

f32, i32, bf16 = jnp.float32, jnp.int32, jnp.bfloat16
AXES = ("row", "rep")
MESH = pl.DeviceIdType.MESH
ROWS = 5
UNIT = 4096
STEP = 64


def iota(shape, dim):
    return lax.broadcasted_iota(i32, shape, dim)


def pick(cond):
    return jnp.where(cond, 1.0, 0.0).astype(bf16)


def bytes_of(code):
    return (code >> 8).astype(f32).astype(bf16), (code & 255).astype(f32).astype(bf16)


def joined(parts):
    y = (parts[:, 0:128] * 256.0 + parts[:, 128:256]).astype(i32)
    x = (parts[:, 256:384] * 256.0 + parts[:, 384:512]).astype(i32)
    return (y << 16) | (x & 65535)


def place_of(piece):
    return {"row": piece // 2, "rep": piece % 2}


def exchange(
    winds_hbm, owner_hbm, tracers_hbm, words, spread,
    winds, owner, tracers, low, high, parts, snd, rcv, every, where,
    send_sem, recv_sem, halo_send, halo_recv, pass_send, pass_recv, load_sem,
):
    pieces = snd.shape[0]
    blocks = words.shape[0]
    edge = low.shape[0]
    share = blocks // 4
    me = lax.axis_index(AXES)
    col = lax.axis_index("col")
    after = lax.rem(me + 1, pieces)
    before = lax.rem(me + pieces - 1, pieces)

    barrier = pltpu.get_barrier_semaphore()

    def greet(i, _):
        to = lax.rem(me + i, pieces)
        pl.semaphore_signal(barrier, inc=1, device_id=place_of(to), device_id_type=MESH)
        return 0

    lax.fori_loop(1, pieces, greet, 0)
    for c in range(1, 4):
        peer = {"col": lax.rem(col + c, 4)}
        pl.semaphore_signal(barrier, inc=1, device_id=peer, device_id_type=MESH)

    load_owner = pltpu.make_async_copy(owner_hbm, owner, load_sem.at[0])
    load_winds = pltpu.make_async_copy(winds_hbm, winds, load_sem.at[1])
    load_tracers = pltpu.make_async_copy(tracers_hbm, tracers, load_sem.at[2])
    load_owner.start()
    load_winds.start()
    load_tracers.start()

    load_owner.wait()
    lanes = iota((128, 128), 1)
    step = jnp.concatenate([pick(iota((128, 128), 0) < lanes), jnp.ones((128, 128), bf16)], 1)
    run = jnp.zeros((pieces, 128), f32)
    sums = jnp.zeros((pieces, 128), f32)
    first_lane = lax.rem(me, 32) * 4
    for g in range(blocks // 128):
        own = owner[g : g + 1, :]
        to = own // blocks
        slot = own - to * blocks
        mine = iota((pieces, 128), 0) == to
        hot = pick(mine)
        seen = jnp.dot(hot, step, preferred_element_type=f32)
        rank = jnp.sum(jnp.where(mine, seen[:, :128] + run, 0.0), axis=0, keepdims=True)
        rank = rank.astype(i32) - 4 * col
        run = run + seen[:, 128:]
        here = (rank >= 0) & (rank < 4)
        where[g : g + 1, :] = jnp.where(here, to * 4 + rank, -1)
        lane = iota((128, 128), 0) == jnp.where(here, rank + first_lane, -1)
        for part, scale in ((slot >> 5, 32.0), (slot & 31, 1.0)):
            spot = jnp.where(lane, part.astype(f32), 0.0).astype(bf16)
            sums = sums + scale * lax.dot_general(
                hot, spot, (((1,), (1,)), ((), ())), preferred_element_type=f32
            )
    for d in range(pieces):
        snd[d, 4:5, :] = sums[d : d + 1].astype(i32)

    load_winds.wait()

    def encode(i, _):
        base = i * 64
        y = jnp.concatenate([winds[pl.ds((base + 8 * j) * 2, 8, stride=2), :] for j in range(8)], 0)
        x = jnp.concatenate([winds[pl.ds((base + 8 * j) * 2 + 1, 8, stride=2), :] for j in range(8)], 0)
        cy = jnp.round(jnp.tanh(y) * (6.0 * UNIT)).astype(i32)
        cx = jnp.round(jnp.tanh(x) * (4.0 * UNIT)).astype(i32)
        parts[pl.ds(pl.multiple_of(base, 64), 64), :] = jnp.concatenate(bytes_of(cy) + bytes_of(cx), 1)
        return 0

    lax.fori_loop(0, blocks // 64, encode, 0)

    def one_hot(base, height):
        return jnp.concatenate(
            [pick(iota((height, 128), 0) + base == where[g : g + 1, :]) for g in range(blocks // 128)], 1
        )

    word = joined(jnp.dot(one_hot(0, share), parts[...], preferred_element_type=f32))
    snd[:, 0:4, :] = word.reshape(pieces, 4, 128)

    pl.semaphore_wait(barrier, pieces + 2)

    def message(to, frm):
        return pltpu.make_async_remote_copy(
            src_ref=snd.at[to, pl.ds(0, ROWS)],
            dst_ref=rcv.at[frm, pl.ds(0, ROWS)],
            send_sem=send_sem.at[to],
            recv_sem=recv_sem.at[frm],
            device_id=place_of(to),
            device_id_type=MESH,
        )

    def start(i, _):
        message(lax.rem(me + i, pieces), me).start()
        return 0

    lax.fori_loop(1, pieces, start, 0)

    up = pltpu.make_async_remote_copy(
        src_ref=tracers_hbm.at[pl.ds(tracers.shape[0] - edge, edge)],
        dst_ref=low,
        send_sem=halo_send.at[0],
        recv_sem=halo_recv.at[0],
        device_id=place_of(after),
        device_id_type=MESH,
    )
    down = pltpu.make_async_remote_copy(
        src_ref=tracers_hbm.at[pl.ds(0, edge)],
        dst_ref=high,
        send_sem=halo_send.at[1],
        recv_sem=halo_recv.at[1],
        device_id=place_of(before),
        device_id_type=MESH,
    )
    up.start()
    down.start()
    rcv[me, 0:ROWS, :] = snd[me, 0:ROWS, :]

    own_row = (iota((8, 128), 1) >> 4) == iota((8, 128), 0)

    def widen(ref, first):
        def one(i, _):
            x = ref[pl.ds(pl.multiple_of(i * 32, 32), 32), :].astype(f32)
            y = jnp.where(own_row[None], jnp.broadcast_to(x[:, None, :], (32, 8, 128)), 0.0)
            spread[pl.ds(pl.multiple_of((first + i) * 256, 256), 256), :] = y.reshape(256, 128).astype(bf16)
            return 0

        lax.fori_loop(0, ref.shape[0] // 32, one, 0)

    load_tracers.wait()
    widen(tracers, edge // 32)

    def finish(i, _):
        other = lax.rem(me + i, pieces)
        copy = message(other, other)
        copy.wait_send()
        copy.wait_recv()
        return 0

    lax.fori_loop(1, pieces, finish, 0)

    every[col, 0:share, :] = rcv[:, 0:4, :].reshape(share, 128)
    for h in range(2):
        rows = [rcv[32 * h + s, 4:5, :] for s in range(32)]
        every[col, share + h : share + h + 1, :] = functools.reduce(jnp.add, rows)

    def handed(to, frm):
        return pltpu.make_async_remote_copy(
            src_ref=every.at[col],
            dst_ref=every.at[frm],
            send_sem=pass_send.at[to],
            recv_sem=pass_recv.at[frm],
            device_id={"col": to},
            device_id_type=MESH,
        )

    for c in range(1, 4):
        handed(lax.rem(col + c, 4), col).start()
    for c in range(1, 4):
        other = lax.rem(col + c, 4)
        copy = handed(other, other)
        copy.wait_send()
        copy.wait_recv()

    for c in range(4):
        where[2 * c : 2 * c + 2, :] = every[c, share : share + 2, :]
        for i in range(4):
            word = every[c, 64 * i : 64 * i + 64, :]
            y, x = word >> 16, (word << 16) >> 16
            at = c * share + 64 * i
            parts[at : at + 64, :] = jnp.concatenate(bytes_of(y) + bytes_of(x), 1)

    def settle(i, _):
        base = i * share
        words[pl.ds(pl.multiple_of(base, share), share), :] = joined(
            jnp.dot(one_hot(base, share), parts[...], preferred_element_type=f32)
        )
        return 0

    lax.fori_loop(0, 4, settle, 0)
    up.wait()
    widen(low, 0)
    down.wait()
    widen(high, (edge + tracers.shape[0]) // 32)


def lagrange(t):
    a, b, c = t + 1.0, t - 1.0, t - 2.0
    tb, ac = t * b, a * c
    return tb * c * (-1.0 / 6.0), ac * b * 0.5, ac * t * (-0.5), a * tb * (1.0 / 6.0)


def rows_at(x, index):
    return jnp.take_along_axis(x, index, axis=0, mode="promise_in_bounds")


def folded(a, b, d):
    sub = iota((8, 128), 0)
    mine = (sub & d) == 0
    kept, moved = jnp.where(mine, a, b), jnp.where(mine, b, a)
    return kept + rows_at(moved, sub ^ d)


def transport(dep, words, spread, out, fact_y, fact_x, floors):
    blocks = words.shape[0]
    reach = blocks // 4
    total = blocks * lax.axis_size(AXES)
    shift = reach - lax.axis_index(AXES) * blocks + total
    cell_row = iota((8, 128), 1) >> 4
    cell_col = iota((8, 128), 1) & 15
    sub = iota((8, 128), 0)
    zero = jnp.zeros((8, 128), f32)

    def clear(i, _):
        at = pl.ds(pl.multiple_of(i * 512, 512), 512)
        fact_y[at, :] = jnp.zeros((512, 128), f32)
        fact_x[at, :] = jnp.zeros((512, 128), f32)
        return 0

    lax.fori_loop(0, blocks // 64, clear, 0)

    def factors(i, _):
        for u in range(4):
            g = i * 4 + u
            at = pl.ds(pl.multiple_of(g * 8, 8), 8)
            word = words[at, :]
            pos_y = (cell_row + 8) * UNIT - (word >> 16)
            pos_x = cell_col * UNIT - ((word << 16) >> 16)
            wy = lagrange((pos_y & (UNIT - 1)).astype(f32) * (1.0 / UNIT))
            wx = lagrange((pos_x & (UNIT - 1)).astype(f32) * (1.0 / UNIT))
            for p in range(4):
                fact_y[pl.ds(g * 64 + p, 8, stride=8), :] = wy[p]
                fact_x[pl.ds(g * 64 + p, 8, stride=8), :] = wx[p]
            floors[0, at, :] = pos_y >> 12
            floors[1, at, :] = pos_x >> 12
        return 0

    lax.fori_loop(0, blocks // 32, factors, 0)

    def two_blocks(first):
        prods = []
        for e in (0, 1):
            b = first + e
            lines = []
            for k in range(3):
                d = (dep[k, b] + shift) & (total - 1)
                lines.append(spread[pl.ds(pl.multiple_of(d * 32, 32), 32), :])
            uy = (sub + 1) - jnp.broadcast_to(floors[0, pl.ds(b, 1), :], (8, 128))
            ux = (sub + 1) - jnp.broadcast_to(floors[1, pl.ds(b, 1), :], (8, 128))
            at = pl.ds(pl.multiple_of(b * 8, 8), 8)
            gy = rows_at(fact_y[at, :], uy & 7)
            gx = rows_at(fact_x[at, :], ux & 7)
            near = (ux & 8) == 0
            cols = jnp.concatenate([jnp.where(near, gx, zero), jnp.where(near, zero, gx)], 0).astype(bf16)
            sums = jnp.dot(
                jnp.concatenate(lines, 0), jnp.concatenate([cols] * 8, 0), preferred_element_type=f32
            )
            in0, in1 = uy >= 0, uy >= -8
            for t in range(4):
                r0, r1, r2 = (sums[32 * k + 8 * t : 32 * k + 8 * t + 8] for k in range(3))
                prods.append(jnp.where(in0, r0, jnp.where(in1, r1, r2)) * gy)
        for d in (4, 2, 1):
            prods = [folded(prods[i], prods[i + d], d) for i in range(d)]
        return prods[0]

    def some(i, _):
        for q in range(0, STEP, 4):
            b = i * STEP + q
            four = jnp.concatenate([two_blocks(b), two_blocks(b + 2)], 0).astype(bf16)
            out[pl.ds(pl.multiple_of(b * 4, 16), 16), :] = four
        return 0

    lax.fori_loop(0, blocks // STEP, some, 0)


def in_vmem(n):
    return [pl.BlockSpec(memory_space=pltpu.VMEM)] * n


def on_device(tracers, winds, tile_owner, departure):
    pieces = lax.axis_size(AXES)
    blocks = tile_owner.shape[0]
    panel = tracers.shape[0]
    edge = blocks // 4 * panel
    lines = tracers.reshape(panel, blocks, 128).transpose(1, 0, 2).reshape(blocks * panel, 128)
    wind_lines = winds.reshape(2, blocks, 128).transpose(1, 0, 2).reshape(blocks * 2, 128)
    dma = pltpu.SemaphoreType.DMA
    words, spread = pl.pallas_call(
        exchange,
        out_shape=(
            jax.ShapeDtypeStruct((blocks, 128), i32),
            jax.ShapeDtypeStruct((blocks * 48, 128), bf16),
        ),
        in_specs=[pl.BlockSpec(memory_space=pltpu.HBM)] * 3,
        out_specs=tuple(in_vmem(2)),
        scratch_shapes=[
            pltpu.VMEM((blocks * 2, 128), f32),
            pltpu.VMEM((blocks // 128, 128), i32),
            pltpu.VMEM((blocks * panel, 128), bf16),
            pltpu.VMEM((edge, 128), bf16),
            pltpu.VMEM((edge, 128), bf16),
            pltpu.VMEM((blocks, 512), bf16),
            pltpu.VMEM((pieces, 8, 128), i32),
            pltpu.VMEM((pieces, 8, 128), i32),
            pltpu.VMEM((4, blocks // 4 + 8, 128), i32),
            pltpu.VMEM((8, 128), i32),
            dma((pieces,)),
            dma((pieces,)),
            dma((2,)),
            dma((2,)),
            dma((4,)),
            dma((4,)),
            dma((3,)),
        ],
        compiler_params=pltpu.CompilerParams(
            collective_id=0, has_side_effects=True, vmem_limit_bytes=36 << 20
        ),
    )(wind_lines, tile_owner.reshape(blocks // 128, 128), lines)
    out = pl.pallas_call(
        transport,
        out_shape=jax.ShapeDtypeStruct((blocks * panel, 128), bf16),
        in_specs=[pl.BlockSpec(memory_space=pltpu.SMEM)] + in_vmem(2),
        out_specs=in_vmem(1)[0],
        scratch_shapes=[
            pltpu.VMEM((blocks * 8, 128), f32),
            pltpu.VMEM((blocks * 8, 128), f32),
            pltpu.VMEM((2, blocks, 128), i32),
        ],
        compiler_params=pltpu.CompilerParams(vmem_limit_bytes=36 << 20),
    )(departure.T, words, spread)
    return out.reshape(blocks, panel, 128).transpose(1, 0, 2).reshape(panel, blocks * 128)


def solution(mesh):
    placed = (
        P("col", AXES),
        P(None, AXES),
        P(AXES),
        P(AXES, None),
    )
    return jax.shard_map(
        on_device, mesh=mesh, in_specs=placed, out_specs=P("col", AXES), check_vma=False
    )
```

```python
import functools

import jax
import jax.numpy as jnp
from jax import lax
from jax.experimental import pallas as pl
from jax.experimental.pallas import tpu as pltpu
from jax.sharding import PartitionSpec as P

f32, i32, bf16 = jnp.float32, jnp.int32, jnp.bfloat16
AXES = ("row", "rep")
MESH = pl.DeviceIdType.MESH
ROWS = 5
UNIT = 4096
STEP = 64


def iota(shape, dim):
    return lax.broadcasted_iota(i32, shape, dim)


def pick(cond):
    return jnp.where(cond, 1.0, 0.0).astype(bf16)


def bytes_of(code):
    return (code >> 8).astype(f32).astype(bf16), (code & 255).astype(f32).astype(bf16)


def joined(parts):
    y = (parts[:, 0:128] * 256.0 + parts[:, 128:256]).astype(i32)
    x = (parts[:, 256:384] * 256.0 + parts[:, 384:512]).astype(i32)
    return (y << 16) | (x & 65535)


def place_of(piece):
    return {"row": piece // 2, "rep": piece % 2}


def advect(
    winds_hbm, owner_hbm, tracers_hbm, dep_hbm, out,
    winds, owner, tracers, dep, low, high, parts, snd, rcv, every, where,
    words, spread, fact_y, fact_x, floors,
    send_sem, recv_sem, halo_send, halo_recv, pass_send, pass_recv, load_sem,
):
    pieces = snd.shape[0]
    blocks = words.shape[0]
    edge = low.shape[0]
    share = blocks // 4
    me = lax.axis_index(AXES)
    col = lax.axis_index("col")
    after = lax.rem(me + 1, pieces)
    before = lax.rem(me + pieces - 1, pieces)

    barrier = pltpu.get_barrier_semaphore()

    def greet(i, _):
        to = lax.rem(me + i, pieces)
        pl.semaphore_signal(barrier, inc=1, device_id=place_of(to), device_id_type=MESH)
        return 0

    lax.fori_loop(1, pieces, greet, 0)
    left, right = lax.rem(col + 3, 4), lax.rem(col + 1, 4)
    for c in (left, right):
        pl.semaphore_signal(barrier, inc=1, device_id={"col": c}, device_id_type=MESH)

    load_owner = pltpu.make_async_copy(owner_hbm, owner, load_sem.at[0])
    load_winds = pltpu.make_async_copy(winds_hbm, winds, load_sem.at[1])
    load_tracers = pltpu.make_async_copy(tracers_hbm, tracers, load_sem.at[2])
    load_owner.start()
    load_winds.start()
    load_tracers.start()
    load_dep = pltpu.make_async_copy(dep_hbm, dep, load_sem.at[3])
    load_dep.start()

    load_owner.wait()
    lanes = iota((128, 128), 1)
    step = jnp.concatenate([pick(iota((128, 128), 0) < lanes), jnp.ones((128, 128), bf16)], 1)
    run = jnp.zeros((pieces, 128), f32)
    sums = jnp.zeros((pieces, 128), f32)
    first_lane = lax.rem(me, 32) * 4
    for g in range(blocks // 128):
        own = owner[g : g + 1, :]
        to = own // blocks
        slot = own - to * blocks
        mine = iota((pieces, 128), 0) == to
        hot = pick(mine)
        seen = jnp.dot(hot, step, preferred_element_type=f32)
        rank = jnp.sum(jnp.where(mine, seen[:, :128] + run, 0.0), axis=0, keepdims=True)
        rank = rank.astype(i32) - 4 * col
        run = run + seen[:, 128:]
        here = (rank >= 0) & (rank < 4)
        where[g : g + 1, :] = jnp.where(here, to * 4 + rank, -1)
        lane = iota((128, 128), 0) == jnp.where(here, rank + first_lane, -1)
        for part, scale in ((slot >> 5, 32.0), (slot & 31, 1.0)):
            spot = jnp.where(lane, part.astype(f32), 0.0).astype(bf16)
            sums = sums + scale * lax.dot_general(
                hot, spot, (((1,), (1,)), ((), ())), preferred_element_type=f32
            )
    for d in range(pieces):
        snd[d, 4:5, :] = sums[d : d + 1].astype(i32)

    load_winds.wait()

    def encode(i, _):
        base = i * 64
        y = jnp.concatenate([winds[pl.ds((base + 8 * j) * 2, 8, stride=2), :] for j in range(8)], 0)
        x = jnp.concatenate([winds[pl.ds((base + 8 * j) * 2 + 1, 8, stride=2), :] for j in range(8)], 0)
        cy = jnp.round(jnp.tanh(y) * (6.0 * UNIT)).astype(i32)
        cx = jnp.round(jnp.tanh(x) * (4.0 * UNIT)).astype(i32)
        parts[pl.ds(pl.multiple_of(base, 64), 64), :] = jnp.concatenate(bytes_of(cy) + bytes_of(cx), 1)
        return 0

    lax.fori_loop(0, blocks // 64, encode, 0)

    def one_hot(base, height):
        return jnp.concatenate(
            [pick(iota((height, 128), 0) + base == where[g : g + 1, :]) for g in range(blocks // 128)], 1
        )

    word = joined(jnp.dot(one_hot(0, share), parts[...], preferred_element_type=f32))
    snd[:, 0:4, :] = word.reshape(pieces, 4, 128)

    pl.semaphore_wait(barrier, pieces + 1)

    def message(to, frm):
        return pltpu.make_async_remote_copy(
            src_ref=snd.at[to, pl.ds(0, ROWS)],
            dst_ref=rcv.at[frm, pl.ds(0, ROWS)],
            send_sem=send_sem.at[to],
            recv_sem=recv_sem.at[frm],
            device_id=place_of(to),
            device_id_type=MESH,
        )

    def start(i, _):
        message(lax.rem(me + i, pieces), me).start()
        return 0

    lax.fori_loop(1, pieces, start, 0)

    up = pltpu.make_async_remote_copy(
        src_ref=tracers_hbm.at[pl.ds(tracers.shape[0] - edge, edge)],
        dst_ref=low,
        send_sem=halo_send.at[0],
        recv_sem=halo_recv.at[0],
        device_id=place_of(after),
        device_id_type=MESH,
    )
    down = pltpu.make_async_remote_copy(
        src_ref=tracers_hbm.at[pl.ds(0, edge)],
        dst_ref=high,
        send_sem=halo_send.at[1],
        recv_sem=halo_recv.at[1],
        device_id=place_of(before),
        device_id_type=MESH,
    )
    rcv[me, 0:ROWS, :] = snd[me, 0:ROWS, :]

    own_row = (iota((8, 128), 1) >> 4) == iota((8, 128), 0)

    def widen(ref, first):
        def one(i, _):
            x = ref[pl.ds(pl.multiple_of(i * 32, 32), 32), :].astype(f32)
            y = jnp.where(own_row[None], jnp.broadcast_to(x[:, None, :], (32, 8, 128)), 0.0)
            spread[pl.ds((first + i) * 8, 8)] = y.reshape(8, 32, 128).astype(bf16)
            return 0

        lax.fori_loop(0, ref.shape[0] // 32, one, 0)

    load_tracers.wait()
    widen(tracers, edge // 32)
    clear_factors(fact_y, fact_x)

    def finish(i, _):
        other = lax.rem(me + i, pieces)
        copy = message(other, other)
        copy.wait_send()
        copy.wait_recv()
        return 0

    lax.fori_loop(1, pieces, finish, 0)

    every[col, 0:share, :] = rcv[:, 0:4, :].reshape(share, 128)
    for h in range(2):
        rows = [rcv[32 * h + s, 4:5, :] for s in range(32)]
        every[col, share + h : share + h + 1, :] = functools.reduce(jnp.add, rows)

    cut = (share + 8) // 16 * 8 + 8

    def handed(origin, half, to, send):
        at = pl.ds(0, cut) if half == 0 else pl.ds(cut, share + 8 - cut)
        return pltpu.make_async_remote_copy(
            src_ref=every.at[origin, at],
            dst_ref=every.at[origin, at],
            send_sem=pass_send.at[send],
            recv_sem=pass_recv.at[origin, half],
            device_id={"col": to},
            device_id_type=MESH,
        )

    far = lax.rem(col + 2, 4)
    sends = [
        handed(col, 0, right, 0),
        handed(col, 1, left, 1),
        handed(col, 1, right, 2),
        handed(col, 0, left, 3),
    ]
    for copy in sends:
        copy.start()
    up.start()
    down.start()
    handed(left, 0, left, 0).wait_recv()
    sends.append(handed(left, 0, right, 4))
    sends[-1].start()
    handed(right, 1, right, 0).wait_recv()
    sends.append(handed(right, 1, left, 5))
    sends[-1].start()
    handed(left, 1, left, 0).wait_recv()
    handed(right, 0, right, 0).wait_recv()
    handed(far, 0, left, 0).wait_recv()
    handed(far, 1, right, 0).wait_recv()
    for copy in sends:
        copy.wait_send()

    for c in range(4):
        where[2 * c : 2 * c + 2, :] = every[c, share : share + 2, :]
        for i in range(4):
            word = every[c, 64 * i : 64 * i + 64, :]
            y, x = word >> 16, (word << 16) >> 16
            at = c * share + 64 * i
            parts[at : at + 64, :] = jnp.concatenate(bytes_of(y) + bytes_of(x), 1)

    def settle(i, _):
        base = i * share
        words[pl.ds(pl.multiple_of(base, share), share), :] = joined(
            jnp.dot(one_hot(base, share), parts[...], preferred_element_type=f32)
        )
        return 0

    lax.fori_loop(0, 4, settle, 0)
    load_dep.wait()
    step_of = transport(dep, words, spread, out, fact_y, fact_x, floors)
    steps = blocks // STEP
    side = steps // 4

    lax.fori_loop(side, steps - side, step_of, 0)
    up.wait()
    widen(low, 0)
    down.wait()
    widen(high, (edge + tracers.shape[0]) // 32)

    def outer(i, _):
        return step_of(i + (i // side) * (steps // 2), 0)

    lax.fori_loop(0, 2 * side, outer, 0)


def clear_factors(fact_y, fact_x):
    def clear(i, _):
        at = pl.ds(pl.multiple_of(i * 512, 512), 512)
        fact_y[at, :] = jnp.zeros((512, 128), f32)
        fact_x[at, :] = jnp.zeros((512, 128), f32)
        return 0

    lax.fori_loop(0, fact_y.shape[0] // 512, clear, 0)


def lagrange(t):
    a, b, c = t + 1.0, t - 1.0, t - 2.0
    tb, ac = t * b, a * c
    return tb * c * (-1.0 / 6.0), ac * b * 0.5, ac * t * (-0.5), a * tb * (1.0 / 6.0)


def rows_at(x, index):
    return jnp.take_along_axis(x, index, axis=0, mode="promise_in_bounds")


def folded(a, b, d):
    sub = iota((8, 128), 0)
    mine = (sub & d) == 0
    kept, moved = jnp.where(mine, a, b), jnp.where(mine, b, a)
    return kept + rows_at(moved, sub ^ d)


def transport(dep, words, spread, out, fact_y, fact_x, floors):
    blocks = words.shape[0]
    reach = blocks // 4
    total = blocks * lax.axis_size(AXES)
    shift = reach - lax.axis_index(AXES) * blocks + total
    cell_row = iota((8, 128), 1) >> 4
    cell_col = iota((8, 128), 1) & 15
    sub = iota((8, 128), 0)
    zero = jnp.zeros((8, 128), f32)

    def factors(i, _):
        for u in range(4):
            g = i * 4 + u
            at = pl.ds(pl.multiple_of(g * 8, 8), 8)
            word = words[at, :]
            pos_y = (cell_row + 8) * UNIT - (word >> 16)
            pos_x = cell_col * UNIT - ((word << 16) >> 16)
            wy = lagrange((pos_y & (UNIT - 1)).astype(f32) * (1.0 / UNIT))
            wx = lagrange((pos_x & (UNIT - 1)).astype(f32) * (1.0 / UNIT))
            for p in range(4):
                fact_y[pl.ds(g * 64 + p, 8, stride=8), :] = wy[p]
                fact_x[pl.ds(g * 64 + p, 8, stride=8), :] = wx[p]
            floors[0, at, :] = pos_y >> 12
            floors[1, at, :] = pos_x >> 12
        return 0

    lax.fori_loop(0, blocks // 32, factors, 0)

    def two_blocks(first):
        prods = []
        for e in (0, 1):
            b = first + e
            lines = []
            for k in range(3):
                d = jnp.minimum((dep[k, b] + shift) & (total - 1), blocks + 2 * reach - 1)
                lines.append(spread[d])
            uy = (sub + 1) - jnp.broadcast_to(floors[0, pl.ds(b, 1), :], (8, 128))
            ux = (sub + 1) - jnp.broadcast_to(floors[1, pl.ds(b, 1), :], (8, 128))
            at = pl.ds(pl.multiple_of(b * 8, 8), 8)
            gy = rows_at(fact_y[at, :], uy & 7)
            gx = rows_at(fact_x[at, :], ux & 7)
            near = (ux & 8) == 0
            cols = jnp.concatenate([jnp.where(near, gx, zero), jnp.where(near, zero, gx)], 0).astype(bf16)
            sums = jnp.dot(
                jnp.concatenate(lines, 0), jnp.concatenate([cols] * 8, 0), preferred_element_type=f32
            )
            in0, in1 = uy >= 0, uy >= -8
            for t in range(4):
                r0, r1, r2 = (sums[32 * k + 8 * t : 32 * k + 8 * t + 8] for k in range(3))
                prods.append(jnp.where(in0, r0, jnp.where(in1, r1, r2)) * gy)
        for d in (4, 2, 1):
            prods = [folded(prods[i], prods[i + d], d) for i in range(d)]
        return prods[0]

    def some(i, _):
        for q in range(0, STEP, 4):
            b = i * STEP + q
            four = jnp.concatenate([two_blocks(b), two_blocks(b + 2)], 0).astype(bf16)
            out[pl.ds(pl.multiple_of(b * 4, 16), 16), :] = four
        return 0

    return some


def on_device(tracers, winds, tile_owner, departure):
    pieces = lax.axis_size(AXES)
    blocks = tile_owner.shape[0]
    panel = tracers.shape[0]
    edge = blocks // 4 * panel
    lines = tracers.reshape(panel, blocks, 128).transpose(1, 0, 2).reshape(blocks * panel, 128)
    wind_lines = winds.reshape(2, blocks, 128).transpose(1, 0, 2).reshape(blocks * 2, 128)
    dma = pltpu.SemaphoreType.DMA
    out = pl.pallas_call(
        advect,
        out_shape=jax.ShapeDtypeStruct((blocks * panel, 128), bf16),
        in_specs=[pl.BlockSpec(memory_space=pltpu.HBM)] * 4,
        out_specs=pl.BlockSpec(memory_space=pltpu.VMEM),
        scratch_shapes=[
            pltpu.VMEM((blocks * 2, 128), f32),
            pltpu.VMEM((blocks // 128, 128), i32),
            pltpu.VMEM((blocks * panel, 128), bf16),
            pltpu.SMEM((3, blocks), i32),
            pltpu.VMEM((edge, 128), bf16),
            pltpu.VMEM((edge, 128), bf16),
            pltpu.VMEM((blocks, 512), bf16),
            pltpu.VMEM((pieces, 8, 128), i32),
            pltpu.VMEM((pieces, 8, 128), i32),
            pltpu.VMEM((4, blocks // 4 + 8, 128), i32),
            pltpu.VMEM((8, 128), i32),
            pltpu.VMEM((blocks, 128), i32),
            pltpu.VMEM((blocks * 3 // 2, 32, 128), bf16),
            pltpu.VMEM((blocks * 8, 128), f32),
            pltpu.VMEM((blocks * 8, 128), f32),
            pltpu.VMEM((2, blocks, 128), i32),
            dma((pieces,)),
            dma((pieces,)),
            dma((2,)),
            dma((2,)),
            dma((6,)),
            dma((4, 2)),
            dma((4,)),
        ],
        compiler_params=pltpu.CompilerParams(
            collective_id=0, has_side_effects=True, vmem_limit_bytes=60 << 20
        ),
    )(wind_lines, tile_owner.reshape(blocks // 128, 128), lines, departure.T)
    return out.reshape(blocks, panel, 128).transpose(1, 0, 2).reshape(panel, blocks * 128)


def solution(mesh):
    placed = (
        P("col", AXES),
        P(None, AXES),
        P(AXES),
        P(AXES, None),
    )
    return jax.shard_map(
        on_device, mesh=mesh, in_specs=placed, out_specs=P("col", AXES), check_vma=False
    )
```

```python
import functools

import jax
import jax.numpy as jnp
from jax import lax
from jax.experimental import pallas as pl
from jax.experimental.pallas import tpu as pltpu
from jax.sharding import PartitionSpec as P

f32, i32, bf16 = jnp.float32, jnp.int32, jnp.bfloat16
AXES = ("row", "rep")
MESH = pl.DeviceIdType.MESH
ROWS = 5
UNIT = 4096
STEP = 64


def iota(shape, dim):
    return lax.broadcasted_iota(i32, shape, dim)


def pick(cond):
    return jnp.where(cond, 1.0, 0.0).astype(bf16)


def bytes_of(code):
    return (code >> 8).astype(f32).astype(bf16), (code & 255).astype(f32).astype(bf16)


def joined(parts):
    y = (parts[:, 0:128] * 256.0 + parts[:, 128:256]).astype(i32)
    x = (parts[:, 256:384] * 256.0 + parts[:, 384:512]).astype(i32)
    return (y << 16) | (x & 65535)


def place_of(piece):
    return {"row": piece // 2, "rep": piece % 2}


def advect(
    winds_hbm, owner_hbm, tracers_hbm, dep_hbm, out,
    winds, owner, tracers, dep, low, high, parts, snd, rcv, every, where,
    words, spread, fact_y, fact_x, floors,
    send_sem, recv_sem, halo_send, halo_recv, pass_send, pass_recv, load_sem,
):
    pieces = snd.shape[0]
    blocks = words.shape[0]
    edge = low.shape[0]
    share = blocks // 4
    me = lax.axis_index(AXES)
    col = lax.axis_index("col")
    after = lax.rem(me + 1, pieces)
    before = lax.rem(me + pieces - 1, pieces)

    barrier = pltpu.get_barrier_semaphore()

    def greet(i, _):
        to = lax.rem(me + i, pieces)
        pl.semaphore_signal(barrier, inc=1, device_id=place_of(to), device_id_type=MESH)
        return 0

    lax.fori_loop(1, pieces, greet, 0)
    left, right = lax.rem(col + 3, 4), lax.rem(col + 1, 4)
    for c in (left, right):
        pl.semaphore_signal(barrier, inc=1, device_id={"col": c}, device_id_type=MESH)

    load_owner = pltpu.make_async_copy(owner_hbm, owner, load_sem.at[0])
    load_winds = pltpu.make_async_copy(winds_hbm, winds, load_sem.at[1])
    load_tracers = pltpu.make_async_copy(tracers_hbm, tracers, load_sem.at[2])
    load_owner.start()
    load_winds.start()
    load_tracers.start()
    load_dep = pltpu.make_async_copy(dep_hbm, dep, load_sem.at[3])
    load_dep.start()

    load_owner.wait()
    lanes = iota((128, 128), 1)
    step = jnp.concatenate([pick(iota((128, 128), 0) < lanes), jnp.ones((128, 128), bf16)], 1)
    run = jnp.zeros((pieces, 128), f32)
    sums = jnp.zeros((pieces, 128), f32)
    first_lane = lax.rem(me, 32) * 4
    for g in range(blocks // 128):
        own = owner[g : g + 1, :]
        to = own // blocks
        slot = own - to * blocks
        mine = iota((pieces, 128), 0) == to
        hot = pick(mine)
        seen = jnp.dot(hot, step, preferred_element_type=f32)
        rank = jnp.sum(jnp.where(mine, seen[:, :128] + run, 0.0), axis=0, keepdims=True)
        rank = rank.astype(i32) - 4 * col
        run = run + seen[:, 128:]
        here = (rank >= 0) & (rank < 4)
        where[g : g + 1, :] = jnp.where(here, to * 4 + rank, -1)
        lane = iota((128, 128), 0) == jnp.where(here, rank + first_lane, -1)
        for part, scale in ((slot >> 5, 32.0), (slot & 31, 1.0)):
            spot = jnp.where(lane, part.astype(f32), 0.0).astype(bf16)
            sums = sums + scale * lax.dot_general(
                hot, spot, (((1,), (1,)), ((), ())), preferred_element_type=f32
            )
    for d in range(pieces):
        snd[d, 4:5, :] = sums[d : d + 1].astype(i32)

    load_winds.wait()

    def encode(i, _):
        base = i * 64
        y = jnp.concatenate([winds[pl.ds((base + 8 * j) * 2, 8, stride=2), :] for j in range(8)], 0)
        x = jnp.concatenate([winds[pl.ds((base + 8 * j) * 2 + 1, 8, stride=2), :] for j in range(8)], 0)
        cy = jnp.round(jnp.tanh(y) * (6.0 * UNIT)).astype(i32)
        cx = jnp.round(jnp.tanh(x) * (4.0 * UNIT)).astype(i32)
        parts[pl.ds(pl.multiple_of(base, 64), 64), :] = jnp.concatenate(bytes_of(cy) + bytes_of(cx), 1)
        return 0

    lax.fori_loop(0, blocks // 64, encode, 0)

    def one_hot(base, height):
        return jnp.concatenate(
            [pick(iota((height, 128), 0) + base == where[g : g + 1, :]) for g in range(blocks // 128)], 1
        )

    word = joined(jnp.dot(one_hot(0, share), parts[...], preferred_element_type=f32))
    snd[:, 0:4, :] = word.reshape(pieces, 4, 128)

    pl.semaphore_wait(barrier, pieces + 1)

    def message(to, frm):
        return pltpu.make_async_remote_copy(
            src_ref=snd.at[to, pl.ds(0, ROWS)],
            dst_ref=rcv.at[frm, pl.ds(0, ROWS)],
            send_sem=send_sem.at[to],
            recv_sem=recv_sem.at[frm],
            device_id=place_of(to),
            device_id_type=MESH,
        )

    def start(i, _):
        ahead = 1 + lax.rem(i + pieces // 4, pieces - 1)
        message(lax.rem(me + ahead, pieces), me).start()
        return 0

    lax.fori_loop(0, pieces - 1, start, 0)

    up = pltpu.make_async_remote_copy(
        src_ref=tracers_hbm.at[pl.ds(tracers.shape[0] - edge, edge)],
        dst_ref=low,
        send_sem=halo_send.at[0],
        recv_sem=halo_recv.at[0],
        device_id=place_of(after),
        device_id_type=MESH,
    )
    down = pltpu.make_async_remote_copy(
        src_ref=tracers_hbm.at[pl.ds(0, edge)],
        dst_ref=high,
        send_sem=halo_send.at[1],
        recv_sem=halo_recv.at[1],
        device_id=place_of(before),
        device_id_type=MESH,
    )
    rcv[me, 0:ROWS, :] = snd[me, 0:ROWS, :]

    own_row = (iota((8, 128), 1) >> 4) == iota((8, 128), 0)

    def widen(ref, first):
        def one(i, _):
            x = ref[pl.ds(pl.multiple_of(i * 32, 32), 32), :].astype(f32)
            y = jnp.where(own_row[None], jnp.broadcast_to(x[:, None, :], (32, 8, 128)), 0.0)
            spread[pl.ds((first + i) * 8, 8)] = y.reshape(8, 32, 128).astype(bf16)
            return 0

        lax.fori_loop(0, ref.shape[0] // 32, one, 0)

    load_tracers.wait()
    widen(tracers, edge // 32)
    clear_factors(fact_y, fact_x)

    def finish(i, _):
        other = lax.rem(me + i, pieces)
        message(other, other).wait_recv()
        return 0

    lax.fori_loop(1, pieces, finish, 0)

    every[col, 0:share, :] = rcv[:, 0:4, :].reshape(share, 128)
    for h in range(2):
        rows = [rcv[32 * h + s, 4:5, :] for s in range(32)]
        every[col, share + h : share + h + 1, :] = functools.reduce(jnp.add, rows)

    cut = (share + 8) // 16 * 8 + 8

    def handed(origin, half, to, send):
        at = pl.ds(0, cut) if half == 0 else pl.ds(cut, share + 8 - cut)
        return pltpu.make_async_remote_copy(
            src_ref=every.at[origin, at],
            dst_ref=every.at[origin, at],
            send_sem=pass_send.at[send],
            recv_sem=pass_recv.at[origin, half],
            device_id={"col": to},
            device_id_type=MESH,
        )

    far = lax.rem(col + 2, 4)
    sends = [
        handed(col, 0, right, 0),
        handed(col, 1, left, 1),
        handed(col, 1, right, 2),
        handed(col, 0, left, 3),
    ]
    for copy in sends:
        copy.start()
    up.start()
    down.start()
    handed(left, 0, left, 0).wait_recv()
    sends.append(handed(left, 0, right, 4))
    sends[-1].start()
    handed(right, 1, right, 0).wait_recv()
    sends.append(handed(right, 1, left, 5))
    sends[-1].start()
    handed(left, 1, left, 0).wait_recv()
    handed(right, 0, right, 0).wait_recv()
    handed(far, 0, left, 0).wait_recv()
    handed(far, 1, right, 0).wait_recv()

    for c in range(4):
        where[2 * c : 2 * c + 2, :] = every[c, share : share + 2, :]
        for i in range(4):
            word = every[c, 64 * i : 64 * i + 64, :]
            y, x = word >> 16, (word << 16) >> 16
            at = c * share + 64 * i
            parts[at : at + 64, :] = jnp.concatenate(bytes_of(y) + bytes_of(x), 1)

    def settle(i, _):
        base = i * 512
        words[pl.ds(pl.multiple_of(base, 512), 512), :] = joined(
            jnp.dot(one_hot(base, 512), parts[...], preferred_element_type=f32)
        )
        return 0

    lax.fori_loop(0, 2, settle, 0)
    load_dep.wait()
    step_of = transport(dep, words, spread, out, fact_y, fact_x, floors)
    steps = blocks // STEP
    side = steps // 4

    lax.fori_loop(side, steps - side, step_of, 0)
    up.wait()
    widen(low, 0)
    down.wait()
    widen(high, (edge + tracers.shape[0]) // 32)

    def outer(i, _):
        return step_of(i + (i // side) * (steps // 2), 0)

    lax.fori_loop(0, 2 * side, outer, 0)

    def sent(i, _):
        message(lax.rem(me + i, pieces), me).wait_send()
        return 0

    lax.fori_loop(1, pieces, sent, 0)
    for copy in sends:
        copy.wait_send()


def hand_out(whole, out, sems):
    piece = out.shape[0] // 4
    copies = [
        pltpu.make_async_copy(
            whole.at[pl.ds(i * piece, piece)], out.at[pl.ds(i * piece, piece)], sems.at[i]
        )
        for i in range(4)
    ]
    for copy in copies:
        copy.start()
    for copy in copies:
        copy.wait()


def clear_factors(fact_y, fact_x):
    def clear(i, _):
        at = pl.ds(pl.multiple_of(i * 512, 512), 512)
        fact_y[at, :] = jnp.zeros((512, 128), f32)
        fact_x[at, :] = jnp.zeros((512, 128), f32)
        return 0

    lax.fori_loop(0, fact_y.shape[0] // 512, clear, 0)


def lagrange(t):
    a, b, c = t + 1.0, t - 1.0, t - 2.0
    tb, ac = t * b, a * c
    return tb * c * (-1.0 / 6.0), ac * b * 0.5, ac * t * (-0.5), a * tb * (1.0 / 6.0)


def rows_at(x, index):
    return jnp.take_along_axis(x, index, axis=0, mode="promise_in_bounds")


def folded(a, b, d):
    sub = iota((8, 128), 0)
    mine = (sub & d) == 0
    kept, moved = jnp.where(mine, a, b), jnp.where(mine, b, a)
    return kept + rows_at(moved, sub ^ d)


def transport(dep, words, spread, out, fact_y, fact_x, floors):
    blocks = words.shape[0]
    reach = blocks // 4
    total = blocks * lax.axis_size(AXES)
    shift = reach - lax.axis_index(AXES) * blocks + total
    cell_row = iota((8, 128), 1) >> 4
    cell_col = iota((8, 128), 1) & 15
    sub = iota((8, 128), 0)
    zero = jnp.zeros((8, 128), f32)

    def factors(i, _):
        for u in range(4):
            g = i * 4 + u
            at = pl.ds(pl.multiple_of(g * 8, 8), 8)
            word = words[at, :]
            pos_y = (cell_row + 8) * UNIT - (word >> 16)
            pos_x = cell_col * UNIT - ((word << 16) >> 16)
            wy = lagrange((pos_y & (UNIT - 1)).astype(f32) * (1.0 / UNIT))
            wx = lagrange((pos_x & (UNIT - 1)).astype(f32) * (1.0 / UNIT))
            for p in range(4):
                fact_y[pl.ds(g * 64 + p, 8, stride=8), :] = wy[p]
                fact_x[pl.ds(g * 64 + p, 8, stride=8), :] = wx[p]
            floors[0, at, :] = pos_y >> 12
            floors[1, at, :] = pos_x >> 12
        return 0

    lax.fori_loop(0, blocks // 32, factors, 0)

    def two_blocks(first):
        prods = []
        for e in (0, 1):
            b = first + e
            lines = []
            for k in range(3):
                d = jnp.minimum((dep[k, b] + shift) & (total - 1), blocks + 2 * reach - 1)
                lines.append(spread[d])
            uy = (sub + 1) - jnp.broadcast_to(floors[0, pl.ds(b, 1), :], (8, 128))
            ux = (sub + 1) - jnp.broadcast_to(floors[1, pl.ds(b, 1), :], (8, 128))
            at = pl.ds(pl.multiple_of(b * 8, 8), 8)
            gy = rows_at(fact_y[at, :], uy & 7)
            gx = rows_at(fact_x[at, :], ux & 7)
            near = (ux & 8) == 0
            cols = jnp.concatenate([jnp.where(near, gx, zero), jnp.where(near, zero, gx)], 0).astype(bf16)
            sums = jnp.dot(
                jnp.concatenate(lines, 0), jnp.concatenate([cols] * 8, 0), preferred_element_type=f32
            )
            in0, in1 = uy >= 0, uy >= -8
            for t in range(4):
                r0, r1, r2 = (sums[32 * k + 8 * t : 32 * k + 8 * t + 8] for k in range(3))
                prods.append(jnp.where(in0, r0, jnp.where(in1, r1, r2)) * gy)
        for d in (4, 2, 1):
            prods = [folded(prods[i], prods[i + d], d) for i in range(d)]
        return prods[0]

    def some(i, _):
        for q in range(0, STEP, 4):
            b = i * STEP + q
            four = jnp.concatenate([two_blocks(b), two_blocks(b + 2)], 0).astype(bf16)
            out[pl.ds(pl.multiple_of(b * 4, 16), 16), :] = four
        return 0

    return some


def on_device(tracers, winds, tile_owner, departure):
    pieces = lax.axis_size(AXES)
    blocks = tile_owner.shape[0]
    panel = tracers.shape[0]
    edge = blocks // 4 * panel
    lines = tracers.reshape(panel, blocks, 128).transpose(1, 0, 2).reshape(blocks * panel, 128)
    wind_lines = winds.reshape(2, blocks, 128).transpose(1, 0, 2).reshape(blocks * 2, 128)
    dma = pltpu.SemaphoreType.DMA
    out = pl.pallas_call(
        advect,
        out_shape=jax.ShapeDtypeStruct((blocks * panel, 128), bf16),
        in_specs=[pl.BlockSpec(memory_space=pltpu.HBM)] * 4,
        out_specs=pl.BlockSpec(memory_space=pltpu.VMEM),
        scratch_shapes=[
            pltpu.VMEM((blocks * 2, 128), f32),
            pltpu.VMEM((blocks // 128, 128), i32),
            pltpu.VMEM((blocks * panel, 128), bf16),
            pltpu.SMEM((3, blocks), i32),
            pltpu.VMEM((edge, 128), bf16),
            pltpu.VMEM((edge, 128), bf16),
            pltpu.VMEM((blocks, 512), bf16),
            pltpu.VMEM((pieces, 8, 128), i32),
            pltpu.VMEM((pieces, 8, 128), i32),
            pltpu.VMEM((4, blocks // 4 + 8, 128), i32),
            pltpu.VMEM((8, 128), i32),
            pltpu.VMEM((blocks, 128), i32),
            pltpu.VMEM((blocks * 3 // 2, 32, 128), bf16),
            pltpu.VMEM((blocks * 8, 128), f32),
            pltpu.VMEM((blocks * 8, 128), f32),
            pltpu.VMEM((2, blocks, 128), i32),
            dma((pieces,)),
            dma((pieces,)),
            dma((2,)),
            dma((2,)),
            dma((6,)),
            dma((4, 2)),
            dma((4,)),
        ],
        compiler_params=pltpu.CompilerParams(
            collective_id=0, has_side_effects=True, vmem_limit_bytes=60 << 20
        ),
    )(wind_lines, tile_owner.reshape(blocks // 128, 128), lines, departure.T)
    out = pl.pallas_call(
        hand_out,
        out_shape=jax.ShapeDtypeStruct(out.shape, bf16),
        in_specs=[pl.BlockSpec(memory_space=pltpu.HBM)],
        out_specs=pl.BlockSpec(memory_space=pltpu.HBM),
        scratch_shapes=[dma((4,))],
        compiler_params=pltpu.CompilerParams(vmem_limit_bytes=60 << 20),
    )(out)
    return out.reshape(blocks, panel, 128).transpose(1, 0, 2).reshape(panel, blocks * 128)


def solution(mesh):
    placed = (
        P("col", AXES),
        P(None, AXES),
        P(AXES),
        P(AXES, None),
    )
    return jax.shard_map(
        on_device, mesh=mesh, in_specs=placed, out_specs=P("col", AXES), check_vma=False
    )
```

```python
import functools

import jax
import jax.numpy as jnp
from jax import lax
from jax.experimental import pallas as pl
from jax.experimental.pallas import tpu as pltpu
from jax.sharding import PartitionSpec as P

f32, i32, bf16 = jnp.float32, jnp.int32, jnp.bfloat16
AXES = ("row", "rep")
MESH = pl.DeviceIdType.MESH
ROWS = 5
UNIT = 4096
STEP = 128


def iota(shape, dim):
    return lax.broadcasted_iota(i32, shape, dim)


def pick(cond):
    return jnp.where(cond, 1.0, 0.0).astype(bf16)


def bytes_of(code):
    return (code >> 8).astype(f32).astype(bf16), (code & 255).astype(f32).astype(bf16)


def joined(parts):
    y = (parts[:, 0:128] * 256.0 + parts[:, 128:256]).astype(i32)
    x = (parts[:, 256:384] * 256.0 + parts[:, 384:512]).astype(i32)
    return (y << 16) | (x & 65535)


def place_of(piece):
    return {"row": piece // 2, "rep": piece % 2}


def advect(
    winds_hbm, owner_hbm, tracers_hbm, dep_hbm, out,
    winds, owner, tracers, dep, low, high, parts, snd, rcv, every, where,
    words, spread, fact_y, fact_x, floors, dep_far, dep_near, cells, out_sem,
    send_sem, recv_sem, halo_send, halo_recv, pass_send, pass_recv, load_sem,
):
    pieces = snd.shape[0]
    blocks = words.shape[0]
    edge = low.shape[0]
    share = blocks // 4
    me = lax.axis_index(AXES)
    col = lax.axis_index("col")
    after = lax.rem(me + 1, pieces)
    before = lax.rem(me + pieces - 1, pieces)

    barrier = pltpu.get_barrier_semaphore()

    def greet(i, _):
        to = lax.rem(me + i, pieces)
        pl.semaphore_signal(barrier, inc=1, device_id=place_of(to), device_id_type=MESH)
        return 0

    lax.fori_loop(1, pieces, greet, 0)
    left, right = lax.rem(col + 3, 4), lax.rem(col + 1, 4)
    for c in (left, right):
        pl.semaphore_signal(barrier, inc=1, device_id={"col": c}, device_id_type=MESH)

    load_owner = pltpu.make_async_copy(owner_hbm, owner, load_sem.at[0])
    load_winds = pltpu.make_async_copy(winds_hbm, winds, load_sem.at[1])
    load_tracers = pltpu.make_async_copy(tracers_hbm, tracers, load_sem.at[2])
    load_owner.start()
    load_winds.start()
    load_tracers.start()
    load_dep = pltpu.make_async_copy(dep_hbm, dep_far, load_sem.at[3])
    load_dep.start()

    load_owner.wait()
    lanes = iota((128, 128), 1)
    step = jnp.concatenate([pick(iota((128, 128), 0) < lanes), jnp.ones((128, 128), bf16)], 1)
    run = jnp.zeros((pieces, 128), f32)
    sums = jnp.zeros((pieces, 128), f32)
    first_lane = lax.rem(me, 32) * 4
    for g in range(blocks // 128):
        own = owner[g : g + 1, :]
        to = own // blocks
        slot = own - to * blocks
        mine = iota((pieces, 128), 0) == to
        hot = pick(mine)
        seen = jnp.dot(hot, step, preferred_element_type=f32)
        rank = jnp.sum(jnp.where(mine, seen[:, :128] + run, 0.0), axis=0, keepdims=True)
        rank = rank.astype(i32) - 4 * col
        run = run + seen[:, 128:]
        here = (rank >= 0) & (rank < 4)
        where[g : g + 1, :] = jnp.where(here, to * 4 + rank, -1)
        lane = iota((128, 128), 0) == jnp.where(here, rank + first_lane, -1)
        for part, scale in ((slot >> 5, 32.0), (slot & 31, 1.0)):
            spot = jnp.where(lane, part.astype(f32), 0.0).astype(bf16)
            sums = sums + scale * lax.dot_general(
                hot, spot, (((1,), (1,)), ((), ())), preferred_element_type=f32
            )
    for d in range(pieces):
        snd[d, 4:5, :] = sums[d : d + 1].astype(i32)

    load_winds.wait()

    def encode(i, _):
        base = i * 64
        y = jnp.concatenate([winds[pl.ds((base + 8 * j) * 2, 8, stride=2), :] for j in range(8)], 0)
        x = jnp.concatenate([winds[pl.ds((base + 8 * j) * 2 + 1, 8, stride=2), :] for j in range(8)], 0)
        cy = jnp.round(jnp.tanh(y) * (6.0 * UNIT)).astype(i32)
        cx = jnp.round(jnp.tanh(x) * (4.0 * UNIT)).astype(i32)
        parts[pl.ds(pl.multiple_of(base, 64), 64), :] = jnp.concatenate(bytes_of(cy) + bytes_of(cx), 1)
        return 0

    lax.fori_loop(0, blocks // 64, encode, 0)

    def one_hot(base, height):
        return jnp.concatenate(
            [pick(iota((height, 128), 0) + base == where[g : g + 1, :]) for g in range(blocks // 128)], 1
        )

    word = joined(jnp.dot(one_hot(0, share), parts[...], preferred_element_type=f32))
    snd[:, 0:4, :] = word.reshape(pieces, 4, 128)

    pl.semaphore_wait(barrier, pieces + 1)

    def message(to, frm):
        return pltpu.make_async_remote_copy(
            src_ref=snd.at[to, pl.ds(0, ROWS)],
            dst_ref=rcv.at[frm, pl.ds(0, ROWS)],
            send_sem=send_sem.at[to],
            recv_sem=recv_sem.at[frm],
            device_id=place_of(to),
            device_id_type=MESH,
        )

    def start(i, _):
        ahead = 1 + lax.rem(i + pieces // 4, pieces - 1)
        message(lax.rem(me + ahead, pieces), me).start()
        return 0

    lax.fori_loop(0, pieces - 1, start, 0)

    up = pltpu.make_async_remote_copy(
        src_ref=tracers_hbm.at[pl.ds(tracers.shape[0] - edge, edge)],
        dst_ref=low,
        send_sem=halo_send.at[0],
        recv_sem=halo_recv.at[0],
        device_id=place_of(after),
        device_id_type=MESH,
    )
    down = pltpu.make_async_remote_copy(
        src_ref=tracers_hbm.at[pl.ds(0, edge)],
        dst_ref=high,
        send_sem=halo_send.at[1],
        recv_sem=halo_recv.at[1],
        device_id=place_of(before),
        device_id_type=MESH,
    )
    rcv[me, 0:ROWS, :] = snd[me, 0:ROWS, :]

    own_row = (iota((8, 128), 1) >> 4) == iota((8, 128), 0)

    def widen(ref, first):
        def one(i, _):
            x = ref[pl.ds(pl.multiple_of(i * 32, 32), 32), :].astype(f32)
            y = jnp.where(own_row[None], jnp.broadcast_to(x[:, None, :], (32, 8, 128)), 0.0)
            spread[pl.ds((first + i) * 8, 8)] = y.reshape(8, 32, 128).astype(bf16)
            return 0

        lax.fori_loop(0, ref.shape[0] // 32, one, 0)

    load_tracers.wait()
    widen(tracers, edge // 32)
    clear_factors(fact_y, fact_x)

    load_dep.wait()
    reach = blocks // 4
    ahead = dep_far[...] - (me * blocks - reach)
    total = blocks * pieces
    ahead = jnp.where(ahead < 0, ahead + total, jnp.where(ahead >= total, ahead - total, ahead))
    dep_near[...] = jnp.clip(ahead, 0, blocks + 2 * reach - 1)
    place_dep = pltpu.make_async_copy(dep_near, dep, load_sem.at[4])
    place_dep.start()

    def finish(i, _):
        other = lax.rem(me + i, pieces)
        message(other, other).wait_recv()
        return 0

    lax.fori_loop(1, pieces, finish, 0)

    every[col, 0:share, :] = rcv[:, 0:4, :].reshape(share, 128)
    for h in range(2):
        rows = [rcv[32 * h + s, 4:5, :] for s in range(32)]
        every[col, share + h : share + h + 1, :] = functools.reduce(jnp.add, rows)

    cut = (share + 8) // 16 * 8 + 8

    def handed(origin, half, to, send):
        at = pl.ds(0, cut) if half == 0 else pl.ds(cut, share + 8 - cut)
        return pltpu.make_async_remote_copy(
            src_ref=every.at[origin, at],
            dst_ref=every.at[origin, at],
            send_sem=pass_send.at[send],
            recv_sem=pass_recv.at[origin, half],
            device_id={"col": to},
            device_id_type=MESH,
        )

    far = lax.rem(col + 2, 4)
    sends = [
        handed(col, 0, right, 0),
        handed(col, 1, left, 1),
        handed(col, 1, right, 2),
        handed(col, 0, left, 3),
    ]
    for copy in sends:
        copy.start()
    up.start()
    down.start()
    handed(left, 0, left, 0).wait_recv()
    sends.append(handed(left, 0, right, 4))
    sends[-1].start()
    handed(right, 1, right, 0).wait_recv()
    sends.append(handed(right, 1, left, 5))
    sends[-1].start()
    handed(left, 1, left, 0).wait_recv()
    handed(right, 0, right, 0).wait_recv()
    handed(far, 0, left, 0).wait_recv()
    handed(far, 1, right, 0).wait_recv()

    for c in range(4):
        where[2 * c : 2 * c + 2, :] = every[c, share : share + 2, :]
        for i in range(4):
            word = every[c, 64 * i : 64 * i + 64, :]
            y, x = word >> 16, (word << 16) >> 16
            at = c * share + 64 * i
            parts[at : at + 64, :] = jnp.concatenate(bytes_of(y) + bytes_of(x), 1)

    def settle(i, _):
        base = i * 512
        words[pl.ds(pl.multiple_of(base, 512), 512), :] = joined(
            jnp.dot(one_hot(base, 512), parts[...], preferred_element_type=f32)
        )
        return 0

    lax.fori_loop(0, 2, settle, 0)
    place_dep.wait()
    step_of = transport(dep, words, spread, cells, fact_y, fact_x, floors)
    steps = blocks // STEP
    side = steps // 4

    lax.fori_loop(side, steps - side, step_of, 0)
    quarter = cells.shape[0] // 4

    def leave(first, count, i):
        at = pl.ds(first * quarter, count * quarter)
        return pltpu.make_async_copy(cells.at[at], out.at[at], out_sem.at[i])

    leave(1, 2, 0).start()
    up.wait()
    widen(low, 0)
    down.wait()
    widen(high, (edge + tracers.shape[0]) // 32)

    def outer(i, _):
        return step_of(i + (i // side) * (steps // 2), 0)

    lax.fori_loop(0, 2 * side, outer, 0)
    leave(0, 1, 1).start()
    leave(3, 1, 2).start()

    def sent(i, _):
        message(lax.rem(me + i, pieces), me).wait_send()
        return 0

    lax.fori_loop(1, pieces, sent, 0)
    for copy in sends:
        copy.wait_send()
    leave(1, 2, 0).wait()
    leave(0, 1, 1).wait()
    leave(3, 1, 2).wait()


def hand_out(whole, out, held, in_sem, out_sem):
    piece = out.shape[0] // 4
    at = [pl.ds(i * piece, piece) for i in range(4)]
    entering = [pltpu.make_async_copy(whole.at[p], held.at[p], in_sem.at[i]) for i, p in enumerate(at)]
    leaving = [pltpu.make_async_copy(held.at[p], out.at[p], out_sem.at[i]) for i, p in enumerate(at)]
    for copy in entering:
        copy.start()
    for first, second in zip(entering, leaving):
        first.wait()
        second.start()
    for copy in leaving:
        copy.wait()


def clear_factors(fact_y, fact_x):
    def clear(i, _):
        at = pl.ds(pl.multiple_of(i * 512, 512), 512)
        fact_y[at, :] = jnp.zeros((512, 128), f32)
        fact_x[at, :] = jnp.zeros((512, 128), f32)
        return 0

    lax.fori_loop(0, fact_y.shape[0] // 512, clear, 0)


def lagrange(t):
    a, b, c = t + 1.0, t - 1.0, t - 2.0
    tb, ac = t * b, a * c
    return tb * c * (-1.0 / 6.0), ac * b * 0.5, ac * t * (-0.5), a * tb * (1.0 / 6.0)


def rows_at(x, index):
    return jnp.take_along_axis(x, index, axis=0, mode="promise_in_bounds")


def folded(a, b, d):
    sub = iota((8, 128), 0)
    mine = (sub & d) == 0
    kept, moved = jnp.where(mine, a, b), jnp.where(mine, b, a)
    return kept + rows_at(moved, sub ^ d)


def transport(dep, words, spread, out, fact_y, fact_x, floors):
    blocks = words.shape[0]
    cell_row = iota((8, 128), 1) >> 4
    cell_col = iota((8, 128), 1) & 15
    sub = iota((8, 128), 0)
    zero = jnp.zeros((8, 128), f32)

    def factors(i, _):
        for u in range(4):
            g = i * 4 + u
            at = pl.ds(pl.multiple_of(g * 8, 8), 8)
            word = words[at, :]
            pos_y = (cell_row + 8) * UNIT - (word >> 16)
            pos_x = cell_col * UNIT - ((word << 16) >> 16)
            wy = lagrange((pos_y & (UNIT - 1)).astype(f32) * (1.0 / UNIT))
            wx = lagrange((pos_x & (UNIT - 1)).astype(f32) * (1.0 / UNIT))
            for p in range(4):
                fact_y[pl.ds(g * 64 + p, 8, stride=8), :] = wy[p]
                fact_x[pl.ds(g * 64 + p, 8, stride=8), :] = wx[p]
            floors[0, at, :] = pos_y >> 12
            floors[1, at, :] = pos_x >> 12
        return 0

    lax.fori_loop(0, blocks // 32, factors, 0)

    def two_blocks(first):
        prods = []
        for e in (0, 1):
            b = first + e
            lines = []
            for k in range(3):
                lines.append(spread[dep[k, b]])
            uy = (sub + 1) - jnp.broadcast_to(floors[0, pl.ds(b, 1), :], (8, 128))
            ux = (sub + 1) - jnp.broadcast_to(floors[1, pl.ds(b, 1), :], (8, 128))
            at = pl.ds(pl.multiple_of(b * 8, 8), 8)
            gy = rows_at(fact_y[at, :], uy & 7)
            gx = rows_at(fact_x[at, :], ux & 7)
            near = (ux & 8) == 0
            cols = jnp.concatenate([jnp.where(near, gx, zero), jnp.where(near, zero, gx)], 0).astype(bf16)
            sums = jnp.dot(
                jnp.concatenate(lines, 0), jnp.concatenate([cols] * 8, 0), preferred_element_type=f32
            )
            in0, in1 = uy >= 0, uy >= -8
            for t in range(4):
                r0, r1, r2 = (sums[32 * k + 8 * t : 32 * k + 8 * t + 8] for k in range(3))
                prods.append(jnp.where(in0, r0, jnp.where(in1, r1, r2)) * gy)
        for d in (4, 2, 1):
            prods = [folded(prods[i], prods[i + d], d) for i in range(d)]
        return prods[0]

    def some(i, _):
        for q in range(0, STEP, 4):
            b = i * STEP + q
            four = jnp.concatenate([two_blocks(b), two_blocks(b + 2)], 0).astype(bf16)
            out[pl.ds(pl.multiple_of(b * 4, 16), 16), :] = four
        return 0

    return some


def on_device(tracers, winds, tile_owner, departure):
    pieces = lax.axis_size(AXES)
    blocks = tile_owner.shape[0]
    panel = tracers.shape[0]
    edge = blocks // 4 * panel
    lines = tracers.reshape(panel, blocks, 128).transpose(1, 0, 2).reshape(blocks * panel, 128)
    wind_lines = winds.reshape(2, blocks, 128).transpose(1, 0, 2).reshape(blocks * 2, 128)
    dma = pltpu.SemaphoreType.DMA
    out = pl.pallas_call(
        advect,
        out_shape=jax.ShapeDtypeStruct((blocks * panel, 128), bf16),
        in_specs=[pl.BlockSpec(memory_space=pltpu.HBM)] * 4,
        out_specs=pl.BlockSpec(memory_space=pltpu.HBM),
        scratch_shapes=[
            pltpu.VMEM((blocks * 2, 128), f32),
            pltpu.VMEM((blocks // 128, 128), i32),
            pltpu.VMEM((blocks * panel, 128), bf16),
            pltpu.SMEM((3, blocks), i32),
            pltpu.VMEM((edge, 128), bf16),
            pltpu.VMEM((edge, 128), bf16),
            pltpu.VMEM((blocks, 512), bf16),
            pltpu.VMEM((pieces, 8, 128), i32),
            pltpu.VMEM((pieces, 8, 128), i32),
            pltpu.VMEM((4, blocks // 4 + 8, 128), i32),
            pltpu.VMEM((8, 128), i32),
            pltpu.VMEM((blocks, 128), i32),
            pltpu.VMEM((blocks * 3 // 2, 32, 128), bf16),
            pltpu.VMEM((blocks * 8, 128), f32),
            pltpu.VMEM((blocks * 8, 128), f32),
            pltpu.VMEM((2, blocks, 128), i32),
            pltpu.VMEM((3, blocks), i32),
            pltpu.VMEM((3, blocks), i32),
            pltpu.VMEM((blocks * panel, 128), bf16),
            dma((3,)),
            dma((pieces,)),
            dma((pieces,)),
            dma((2,)),
            dma((2,)),
            dma((6,)),
            dma((4, 2)),
            dma((5,)),
        ],
        compiler_params=pltpu.CompilerParams(
            collective_id=0, has_side_effects=True, vmem_limit_bytes=60 << 20
        ),
    )(wind_lines, tile_owner.reshape(blocks // 128, 128), lines, departure.T)
    out = pl.pallas_call(
        hand_out,
        out_shape=jax.ShapeDtypeStruct(out.shape, bf16),
        in_specs=[pl.BlockSpec(memory_space=pltpu.HBM)],
        out_specs=pl.BlockSpec(memory_space=pltpu.HBM),
        scratch_shapes=[pltpu.VMEM(out.shape, bf16), dma((4,)), dma((4,))],
        compiler_params=pltpu.CompilerParams(vmem_limit_bytes=60 << 20),
    )(out)
    return out.reshape(blocks, panel, 128).transpose(1, 0, 2).reshape(panel, blocks * 128)


def solution(mesh):
    placed = (
        P("col", AXES),
        P(None, AXES),
        P(AXES),
        P(AXES, None),
    )
    return jax.shard_map(
        on_device, mesh=mesh, in_specs=placed, out_specs=P("col", AXES), check_vma=False
    )
```

```python
import functools

import jax
import jax.numpy as jnp
from jax import lax
from jax.experimental import pallas as pl
from jax.experimental.pallas import tpu as pltpu
from jax.sharding import PartitionSpec as P

f32, i32, bf16 = jnp.float32, jnp.int32, jnp.bfloat16
AXES = ("row", "rep")
MESH = pl.DeviceIdType.MESH
ROWS = 5
UNIT = 4096
STEP = 128


def iota(shape, dim):
    return lax.broadcasted_iota(i32, shape, dim)


def pick(cond):
    return jnp.where(cond, 1.0, 0.0).astype(bf16)


def bytes_of(code):
    return (code >> 8).astype(f32).astype(bf16), (code & 255).astype(f32).astype(bf16)


def joined(parts):
    y = (parts[:, 0:128] * 256.0 + parts[:, 128:256]).astype(i32)
    x = (parts[:, 256:384] * 256.0 + parts[:, 384:512]).astype(i32)
    return (y << 16) | (x & 65535)


def place_of(piece):
    return {"row": piece // 2, "rep": piece % 2}


def advect(
    winds_hbm, owner_hbm, tracers_hbm, dep_hbm, out,
    winds, owner, tracers, dep, low, high, parts, snd, rcv, every, where,
    words, spread, fact_y, fact_x, floors, dep_far, dep_near, cells, out_sem,
    send_sem, recv_sem, halo_send, halo_recv, pass_send, pass_recv, load_sem,
):
    pieces = snd.shape[0]
    blocks = words.shape[0]
    edge = low.shape[0]
    share = blocks // 4
    me = lax.axis_index(AXES)
    col = lax.axis_index("col")
    after = lax.rem(me + 1, pieces)
    before = lax.rem(me + pieces - 1, pieces)

    barrier = pltpu.get_barrier_semaphore()

    def greet(i, _):
        to = lax.rem(me + i, pieces)
        pl.semaphore_signal(barrier, inc=1, device_id=place_of(to), device_id_type=MESH)
        return 0

    lax.fori_loop(1, pieces, greet, 0)
    left, right = lax.rem(col + 3, 4), lax.rem(col + 1, 4)
    for c in (left, right):
        pl.semaphore_signal(barrier, inc=1, device_id={"col": c}, device_id_type=MESH)

    load_owner = pltpu.make_async_copy(owner_hbm, owner, load_sem.at[0])
    load_winds = pltpu.make_async_copy(winds_hbm, winds, load_sem.at[1])
    load_tracers = pltpu.make_async_copy(tracers_hbm, tracers, load_sem.at[2])
    load_owner.start()
    load_winds.start()
    load_tracers.start()
    load_dep = pltpu.make_async_copy(dep_hbm, dep_far, load_sem.at[3])
    load_dep.start()

    load_owner.wait()
    lanes = iota((128, 128), 1)
    step = jnp.concatenate([pick(iota((128, 128), 0) < lanes), jnp.ones((128, 128), bf16)], 1)
    run = jnp.zeros((pieces, 128), f32)
    sums = jnp.zeros((pieces, 128), f32)
    for g in range(blocks // 128):
        own = owner[g : g + 1, :]
        to = own // blocks
        slot = own - to * blocks
        mine = iota((pieces, 128), 0) == to
        hot = pick(mine)
        seen = jnp.dot(hot, step, preferred_element_type=f32)
        rank = jnp.sum(jnp.where(mine, seen[:, :128] + run, 0.0), axis=0, keepdims=True)
        rank = rank.astype(i32) - 4 * col
        run = run + seen[:, 128:]
        here = (rank >= 0) & (rank < 4)
        where[g : g + 1, :] = jnp.where(here, to * 4 + rank, -1)
        turn = to - me + (pieces - 1)
        turn = jnp.where(turn >= pieces, turn - pieces, turn)
        lane = iota((128, 128), 0) == jnp.where(here, rank + 4 * (turn & 31), -1)
        for part, scale in ((slot >> 5, 32.0), (slot & 31, 1.0)):
            spot = jnp.where(lane, part.astype(f32), 0.0).astype(bf16)
            sums = sums + scale * lax.dot_general(
                hot, spot, (((1,), (1,)), ((), ())), preferred_element_type=f32
            )
    for d in range(pieces):
        snd[d, 4:5, :] = sums[d : d + 1].astype(i32)

    load_winds.wait()

    def encode(i, _):
        base = i * 64
        y = jnp.concatenate([winds[pl.ds((base + 8 * j) * 2, 8, stride=2), :] for j in range(8)], 0)
        x = jnp.concatenate([winds[pl.ds((base + 8 * j) * 2 + 1, 8, stride=2), :] for j in range(8)], 0)
        cy = jnp.round(jnp.tanh(y) * (6.0 * UNIT)).astype(i32)
        cx = jnp.round(jnp.tanh(x) * (4.0 * UNIT)).astype(i32)
        parts[pl.ds(pl.multiple_of(base, 64), 64), :] = jnp.concatenate(bytes_of(cy) + bytes_of(cx), 1)
        return 0

    lax.fori_loop(0, blocks // 64, encode, 0)

    def one_hot(base, height):
        return jnp.concatenate(
            [pick(iota((height, 128), 0) + base == where[g : g + 1, :]) for g in range(blocks // 128)], 1
        )

    word = joined(jnp.dot(one_hot(0, share), parts[...], preferred_element_type=f32))
    snd[:, 0:4, :] = word.reshape(pieces, 4, 128)

    pl.semaphore_wait(barrier, pieces + 1)

    def message(turn):
        to = lax.rem(me + turn + 1, pieces)
        return pltpu.make_async_remote_copy(
            src_ref=snd.at[to, pl.ds(0, ROWS)],
            dst_ref=rcv.at[turn, pl.ds(0, ROWS)],
            send_sem=send_sem.at[turn],
            recv_sem=recv_sem.at[turn],
            device_id=place_of(to),
            device_id_type=MESH,
        )

    def start(turn, _):
        message(turn).start()
        return 0

    lax.fori_loop(0, pieces - 1, start, 0)

    up = pltpu.make_async_remote_copy(
        src_ref=tracers_hbm.at[pl.ds(tracers.shape[0] - edge, edge)],
        dst_ref=low,
        send_sem=halo_send.at[0],
        recv_sem=halo_recv.at[0],
        device_id=place_of(after),
        device_id_type=MESH,
    )
    down = pltpu.make_async_remote_copy(
        src_ref=tracers_hbm.at[pl.ds(0, edge)],
        dst_ref=high,
        send_sem=halo_send.at[1],
        recv_sem=halo_recv.at[1],
        device_id=place_of(before),
        device_id_type=MESH,
    )
    rcv[pieces - 1, 0:ROWS, :] = snd[me, 0:ROWS, :]

    own_row = (iota((8, 128), 1) >> 4) == iota((8, 128), 0)

    def widen(ref, first):
        def one(i, _):
            x = ref[pl.ds(pl.multiple_of(i * 32, 32), 32), :].astype(f32)
            y = jnp.where(own_row[None], jnp.broadcast_to(x[:, None, :], (32, 8, 128)), 0.0)
            spread[pl.ds((first + i) * 8, 8)] = y.reshape(8, 32, 128).astype(bf16)
            return 0

        lax.fori_loop(0, ref.shape[0] // 32, one, 0)

    load_tracers.wait()
    widen(tracers, edge // 32)
    clear_factors(fact_y, fact_x)

    load_dep.wait()
    reach = blocks // 4
    ahead = dep_far[...] - (me * blocks - reach)
    total = blocks * pieces
    ahead = jnp.where(ahead < 0, ahead + total, jnp.where(ahead >= total, ahead - total, ahead))
    dep_near[...] = jnp.clip(ahead, 0, blocks + 2 * reach - 1)
    place_dep = pltpu.make_async_copy(dep_near, dep, load_sem.at[4])
    place_dep.start()

    def arrive(turn, _):
        message(turn).wait_recv()
        return 0

    far = lax.rem(col + 2, 4)

    def gather(half):
        at = pl.ds(32 * half, 32)
        every[col, half, 0:128, :] = rcv[at, 0:4, :].reshape(128, 128)
        rows = [rcv[32 * half + s, 4:5, :] for s in range(32)]
        every[col, half, 128:129, :] = functools.reduce(jnp.add, rows)

    def handed(origin, half, to, send):
        return pltpu.make_async_remote_copy(
            src_ref=every.at[origin, half],
            dst_ref=every.at[origin, half],
            send_sem=pass_send.at[send],
            recv_sem=pass_recv.at[origin, half],
            device_id={"col": to},
            device_id_type=MESH,
        )

    def unpack(origin, half):
        where[pl.ds(2 * origin + half, 1), :] = every[origin, half, 128:129, :]
        for i in range(2):
            word = every[origin, half, 64 * i : 64 * i + 64, :]
            y, x = word >> 16, (word << 16) >> 16
            at = pl.ds(pl.multiple_of(origin * share + half * 128 + 64 * i, 64), 64)
            parts[at, :] = jnp.concatenate(bytes_of(y) + bytes_of(x), 1)

    lax.fori_loop(0, 32, arrive, 0)
    gather(0)
    sends = [handed(col, 0, right, 0), handed(col, 0, left, 1)]
    sends[0].start()
    sends[1].start()
    unpack(col, 0)
    handed(left, 0, left, 0).wait_recv()
    sends.append(handed(left, 0, right, 2))
    sends[2].start()
    unpack(left, 0)
    lax.fori_loop(32, pieces - 1, arrive, 0)
    gather(1)
    sends += [handed(col, 1, left, 3), handed(col, 1, right, 4)]
    sends[3].start()
    sends[4].start()
    up.start()
    down.start()
    unpack(col, 1)
    handed(right, 0, right, 0).wait_recv()
    unpack(right, 0)
    handed(right, 1, right, 0).wait_recv()
    sends.append(handed(right, 1, left, 5))
    sends[5].start()
    unpack(right, 1)
    handed(left, 1, left, 0).wait_recv()
    unpack(left, 1)
    handed(far, 0, left, 0).wait_recv()
    unpack(far, 0)
    handed(far, 1, right, 0).wait_recv()
    unpack(far, 1)

    def settle(i, _):
        base = i * 512
        words[pl.ds(pl.multiple_of(base, 512), 512), :] = joined(
            jnp.dot(one_hot(base, 512), parts[...], preferred_element_type=f32)
        )
        return 0

    lax.fori_loop(0, 2, settle, 0)
    place_dep.wait()
    step_of = transport(dep, words, spread, cells, fact_y, fact_x, floors)
    steps = blocks // STEP
    side = steps // 4

    lax.fori_loop(side, steps - side, step_of, 0)
    quarter = cells.shape[0] // 4

    def leave(first, count, i):
        at = pl.ds(first * quarter, count * quarter)
        return pltpu.make_async_copy(cells.at[at], out.at[at], out_sem.at[i])

    leave(1, 2, 0).start()
    up.wait()
    widen(low, 0)
    down.wait()
    widen(high, (edge + tracers.shape[0]) // 32)

    def outer(i, _):
        return step_of(i + (i // side) * (steps // 2), 0)

    lax.fori_loop(0, 2 * side, outer, 0)
    leave(0, 1, 1).start()
    leave(3, 1, 2).start()

    def sent(turn, _):
        message(turn).wait_send()
        return 0

    lax.fori_loop(0, pieces - 1, sent, 0)
    for copy in sends:
        copy.wait_send()
    leave(1, 2, 0).wait()
    leave(0, 1, 1).wait()
    leave(3, 1, 2).wait()


def hand_out(whole, out, held, in_sem, out_sem):
    piece = out.shape[0] // 4
    at = [pl.ds(i * piece, piece) for i in range(4)]
    entering = [pltpu.make_async_copy(whole.at[p], held.at[p], in_sem.at[i]) for i, p in enumerate(at)]
    leaving = [pltpu.make_async_copy(held.at[p], out.at[p], out_sem.at[i]) for i, p in enumerate(at)]
    for copy in entering:
        copy.start()
    for first, second in zip(entering, leaving):
        first.wait()
        second.start()
    for copy in leaving:
        copy.wait()


def clear_factors(fact_y, fact_x):
    def clear(i, _):
        at = pl.ds(pl.multiple_of(i * 512, 512), 512)
        fact_y[at, :] = jnp.zeros((512, 128), f32)
        fact_x[at, :] = jnp.zeros((512, 128), f32)
        return 0

    lax.fori_loop(0, fact_y.shape[0] // 512, clear, 0)


def lagrange(t):
    a, b, c = t + 1.0, t - 1.0, t - 2.0
    tb, ac = t * b, a * c
    return tb * c * (-1.0 / 6.0), ac * b * 0.5, ac * t * (-0.5), a * tb * (1.0 / 6.0)


def rows_at(x, index):
    return jnp.take_along_axis(x, index, axis=0, mode="promise_in_bounds")


def folded(a, b, d):
    sub = iota((8, 128), 0)
    mine = (sub & d) == 0
    kept, moved = jnp.where(mine, a, b), jnp.where(mine, b, a)
    return kept + rows_at(moved, sub ^ d)


def transport(dep, words, spread, out, fact_y, fact_x, floors):
    blocks = words.shape[0]
    cell_row = iota((8, 128), 1) >> 4
    cell_col = iota((8, 128), 1) & 15
    sub = iota((8, 128), 0)
    zero = jnp.zeros((8, 128), f32)

    def factors(i, _):
        for u in range(4):
            g = i * 4 + u
            at = pl.ds(pl.multiple_of(g * 8, 8), 8)
            word = words[at, :]
            pos_y = (cell_row + 8) * UNIT - (word >> 16)
            pos_x = cell_col * UNIT - ((word << 16) >> 16)
            wy = lagrange((pos_y & (UNIT - 1)).astype(f32) * (1.0 / UNIT))
            wx = lagrange((pos_x & (UNIT - 1)).astype(f32) * (1.0 / UNIT))
            for p in range(4):
                fact_y[pl.ds(g * 64 + p, 8, stride=8), :] = wy[p]
                fact_x[pl.ds(g * 64 + p, 8, stride=8), :] = wx[p]
            floors[0, at, :] = pos_y >> 12
            floors[1, at, :] = pos_x >> 12
        return 0

    lax.fori_loop(0, blocks // 32, factors, 0)

    def two_blocks(first):
        prods = []
        for e in (0, 1):
            b = first + e
            lines = []
            for k in range(3):
                lines.append(spread[dep[k, b]])
            uy = (sub + 1) - jnp.broadcast_to(floors[0, pl.ds(b, 1), :], (8, 128))
            ux = (sub + 1) - jnp.broadcast_to(floors[1, pl.ds(b, 1), :], (8, 128))
            at = pl.ds(pl.multiple_of(b * 8, 8), 8)
            gy = rows_at(fact_y[at, :], uy & 7)
            gx = rows_at(fact_x[at, :], ux & 7)
            near = (ux & 8) == 0
            cols = jnp.concatenate([jnp.where(near, gx, zero), jnp.where(near, zero, gx)], 0).astype(bf16)
            sums = jnp.dot(
                jnp.concatenate(lines, 0), jnp.concatenate([cols] * 8, 0), preferred_element_type=f32
            )
            in0, in1 = uy >= 0, uy >= -8
            for t in range(4):
                r0, r1, r2 = (sums[32 * k + 8 * t : 32 * k + 8 * t + 8] for k in range(3))
                prods.append(jnp.where(in0, r0, jnp.where(in1, r1, r2)) * gy)
        for d in (4, 2, 1):
            prods = [folded(prods[i], prods[i + d], d) for i in range(d)]
        return prods[0]

    def some(i, _):
        for q in range(0, STEP, 4):
            b = i * STEP + q
            four = jnp.concatenate([two_blocks(b), two_blocks(b + 2)], 0).astype(bf16)
            out[pl.ds(pl.multiple_of(b * 4, 16), 16), :] = four
        return 0

    return some


def on_device(tracers, winds, tile_owner, departure):
    pieces = lax.axis_size(AXES)
    blocks = tile_owner.shape[0]
    panel = tracers.shape[0]
    edge = blocks // 4 * panel
    lines = tracers.reshape(panel, blocks, 128).transpose(1, 0, 2).reshape(blocks * panel, 128)
    wind_lines = winds.reshape(2, blocks, 128).transpose(1, 0, 2).reshape(blocks * 2, 128)
    dma = pltpu.SemaphoreType.DMA
    out = pl.pallas_call(
        advect,
        out_shape=jax.ShapeDtypeStruct((blocks * panel, 128), bf16),
        in_specs=[pl.BlockSpec(memory_space=pltpu.HBM)] * 4,
        out_specs=pl.BlockSpec(memory_space=pltpu.HBM),
        scratch_shapes=[
            pltpu.VMEM((blocks * 2, 128), f32),
            pltpu.VMEM((blocks // 128, 128), i32),
            pltpu.VMEM((blocks * panel, 128), bf16),
            pltpu.SMEM((3, blocks), i32),
            pltpu.VMEM((edge, 128), bf16),
            pltpu.VMEM((edge, 128), bf16),
            pltpu.VMEM((blocks, 512), bf16),
            pltpu.VMEM((pieces, 8, 128), i32),
            pltpu.VMEM((pieces, 8, 128), i32),
            pltpu.VMEM((4, 2, 136, 128), i32),
            pltpu.VMEM((8, 128), i32),
            pltpu.VMEM((blocks, 128), i32),
            pltpu.VMEM((blocks * 3 // 2, 32, 128), bf16),
            pltpu.VMEM((blocks * 8, 128), f32),
            pltpu.VMEM((blocks * 8, 128), f32),
            pltpu.VMEM((2, blocks, 128), i32),
            pltpu.VMEM((3, blocks), i32),
            pltpu.VMEM((3, blocks), i32),
            pltpu.VMEM((blocks * panel, 128), bf16),
            dma((3,)),
            dma((pieces,)),
            dma((pieces,)),
            dma((2,)),
            dma((2,)),
            dma((6,)),
            dma((4, 2)),
            dma((5,)),
        ],
        compiler_params=pltpu.CompilerParams(
            collective_id=0, has_side_effects=True, vmem_limit_bytes=60 << 20
        ),
    )(wind_lines, tile_owner.reshape(blocks // 128, 128), lines, departure.T)
    out = pl.pallas_call(
        hand_out,
        out_shape=jax.ShapeDtypeStruct(out.shape, bf16),
        in_specs=[pl.BlockSpec(memory_space=pltpu.HBM)],
        out_specs=pl.BlockSpec(memory_space=pltpu.HBM),
        scratch_shapes=[pltpu.VMEM(out.shape, bf16), dma((4,)), dma((4,))],
        compiler_params=pltpu.CompilerParams(vmem_limit_bytes=60 << 20),
    )(out)
    return out.reshape(blocks, panel, 128).transpose(1, 0, 2).reshape(panel, blocks * 128)


def solution(mesh):
    placed = (
        P("col", AXES),
        P(None, AXES),
        P(AXES),
        P(AXES, None),
    )
    return jax.shard_map(
        on_device, mesh=mesh, in_specs=placed, out_specs=P("col", AXES), check_vma=False
    )
```

```python
import functools

import jax
import jax.numpy as jnp
from jax import lax
from jax.experimental import pallas as pl
from jax.experimental.pallas import tpu as pltpu
from jax.sharding import PartitionSpec as P

f32, i32, bf16 = jnp.float32, jnp.int32, jnp.bfloat16
AXES = ("row", "rep")
MESH = pl.DeviceIdType.MESH
ROWS = 5
UNIT = 4096
STEP = 128


def iota(shape, dim):
    return lax.broadcasted_iota(i32, shape, dim)


def pick(cond):
    return jnp.where(cond, 1.0, 0.0).astype(bf16)


def bytes_of(code):
    return (code >> 8).astype(f32).astype(bf16), (code & 255).astype(f32).astype(bf16)


def joined(parts):
    y = (parts[:, 0:128] * 256.0 + parts[:, 128:256]).astype(i32)
    x = (parts[:, 256:384] * 256.0 + parts[:, 384:512]).astype(i32)
    return (y << 16) | (x & 65535)


def place_of(piece):
    return {"row": piece // 2, "rep": piece % 2}


def advect(
    winds_hbm, owner_hbm, tracers_hbm, dep_hbm, out,
    winds, owner, tracers, dep, low, high, parts, snd, rcv, every, where,
    words, spread, fact_y, fact_x, floors, dep_far, dep_near, cells, out_sem,
    send_sem, recv_sem, halo_send, halo_recv, pass_send, pass_recv, load_sem,
):
    pieces = snd.shape[0]
    blocks = words.shape[0]
    edge = low.shape[0]
    share = blocks // 4
    me = lax.axis_index(AXES)
    col = lax.axis_index("col")
    after = lax.rem(me + 1, pieces)
    before = lax.rem(me + pieces - 1, pieces)

    barrier = pltpu.get_barrier_semaphore()

    def greet(i, _):
        to = lax.rem(me + i, pieces)
        pl.semaphore_signal(barrier, inc=1, device_id=place_of(to), device_id_type=MESH)
        return 0

    lax.fori_loop(1, pieces, greet, 0)
    left, right = lax.rem(col + 3, 4), lax.rem(col + 1, 4)
    for c in (left, right):
        pl.semaphore_signal(barrier, inc=1, device_id={"col": c}, device_id_type=MESH)

    load_owner = pltpu.make_async_copy(owner_hbm, owner, load_sem.at[0])
    load_winds = pltpu.make_async_copy(winds_hbm, winds, load_sem.at[1])
    load_tracers = pltpu.make_async_copy(tracers_hbm, tracers, load_sem.at[2])
    load_owner.start()
    load_winds.start()
    load_tracers.start()
    load_dep = pltpu.make_async_copy(dep_hbm, dep_far, load_sem.at[3])
    load_dep.start()

    load_owner.wait()
    lanes = iota((128, 128), 1)
    step = jnp.concatenate([pick(iota((128, 128), 0) < lanes), jnp.ones((128, 128), bf16)], 1)
    run = jnp.zeros((pieces, 128), f32)
    sums = jnp.zeros((pieces, 128), f32)
    for g in range(blocks // 128):
        own = owner[g : g + 1, :]
        to = own // blocks
        slot = own - to * blocks
        mine = iota((pieces, 128), 0) == to
        hot = pick(mine)
        seen = jnp.dot(hot, step, preferred_element_type=f32)
        rank = jnp.sum(jnp.where(mine, seen[:, :128] + run, 0.0), axis=0, keepdims=True)
        rank = rank.astype(i32) - 4 * col
        run = run + seen[:, 128:]
        here = (rank >= 0) & (rank < 4)
        where[g : g + 1, :] = jnp.where(here, to * 4 + rank, -1)
        ahead = jnp.where(to >= me, to - me, to - me + pieces)
        turn = ahead - 1 - pieces // 4
        turn = jnp.where(turn < 0, turn + pieces - 1, turn)
        turn = jnp.where(ahead == 0, pieces - 1, turn)
        lane = iota((128, 128), 0) == jnp.where(here, rank + 4 * (turn & 31), -1)
        for part, scale in ((slot >> 5, 32.0), (slot & 31, 1.0)):
            spot = jnp.where(lane, part.astype(f32), 0.0).astype(bf16)
            sums = sums + scale * lax.dot_general(
                hot, spot, (((1,), (1,)), ((), ())), preferred_element_type=f32
            )
    for d in range(pieces):
        snd[d, 4:5, :] = sums[d : d + 1].astype(i32)

    load_winds.wait()

    def encode(i, _):
        base = i * 64
        y = jnp.concatenate([winds[pl.ds((base + 8 * j) * 2, 8, stride=2), :] for j in range(8)], 0)
        x = jnp.concatenate([winds[pl.ds((base + 8 * j) * 2 + 1, 8, stride=2), :] for j in range(8)], 0)
        cy = jnp.round(jnp.tanh(y) * (6.0 * UNIT)).astype(i32)
        cx = jnp.round(jnp.tanh(x) * (4.0 * UNIT)).astype(i32)
        parts[pl.ds(pl.multiple_of(base, 64), 64), :] = jnp.concatenate(bytes_of(cy) + bytes_of(cx), 1)
        return 0

    lax.fori_loop(0, blocks // 64, encode, 0)

    def one_hot(base, height):
        return jnp.concatenate(
            [pick(iota((height, 128), 0) + base == where[g : g + 1, :]) for g in range(blocks // 128)], 1
        )

    word = joined(jnp.dot(one_hot(0, share), parts[...], preferred_element_type=f32))
    snd[:, 0:4, :] = word.reshape(pieces, 4, 128)

    pl.semaphore_wait(barrier, pieces + 1)

    def message(turn):
        to = lax.rem(me + 1 + lax.rem(turn + pieces // 4, pieces - 1), pieces)
        return pltpu.make_async_remote_copy(
            src_ref=snd.at[to, pl.ds(0, ROWS)],
            dst_ref=rcv.at[turn, pl.ds(0, ROWS)],
            send_sem=send_sem.at[turn],
            recv_sem=recv_sem.at[turn],
            device_id=place_of(to),
            device_id_type=MESH,
        )

    def start(turn, _):
        message(turn).start()
        return 0

    lax.fori_loop(0, pieces - 1, start, 0)

    up = pltpu.make_async_remote_copy(
        src_ref=tracers_hbm.at[pl.ds(tracers.shape[0] - edge, edge)],
        dst_ref=low,
        send_sem=halo_send.at[0],
        recv_sem=halo_recv.at[0],
        device_id=place_of(after),
        device_id_type=MESH,
    )
    down = pltpu.make_async_remote_copy(
        src_ref=tracers_hbm.at[pl.ds(0, edge)],
        dst_ref=high,
        send_sem=halo_send.at[1],
        recv_sem=halo_recv.at[1],
        device_id=place_of(before),
        device_id_type=MESH,
    )
    rcv[pieces - 1, 0:ROWS, :] = snd[me, 0:ROWS, :]

    own_row = (iota((8, 128), 1) >> 4) == iota((8, 128), 0)

    def widen(ref, first):
        def one(i, _):
            x = ref[pl.ds(pl.multiple_of(i * 32, 32), 32), :].astype(f32)
            y = jnp.where(own_row[None], jnp.broadcast_to(x[:, None, :], (32, 8, 128)), 0.0)
            spread[pl.ds((first + i) * 8, 8)] = y.reshape(8, 32, 128).astype(bf16)
            return 0

        lax.fori_loop(0, ref.shape[0] // 32, one, 0)

    load_tracers.wait()
    widen(tracers, edge // 32)
    clear_factors(fact_y, fact_x)

    load_dep.wait()
    reach = blocks // 4
    ahead = dep_far[...] - (me * blocks - reach)
    total = blocks * pieces
    ahead = jnp.where(ahead < 0, ahead + total, jnp.where(ahead >= total, ahead - total, ahead))
    dep_near[...] = jnp.clip(ahead, 0, blocks + 2 * reach - 1)
    place_dep = pltpu.make_async_copy(dep_near, dep, load_sem.at[4])
    place_dep.start()

    def arrive(turn, _):
        message(turn).wait_recv()
        return 0

    far = lax.rem(col + 2, 4)

    def gather(half):
        at = pl.ds(32 * half, 32)
        every[col, half, 0:128, :] = rcv[at, 0:4, :].reshape(128, 128)
        rows = [rcv[32 * half + s, 4:5, :] for s in range(32)]
        every[col, half, 128:129, :] = functools.reduce(jnp.add, rows)

    def handed(origin, half, to, send):
        return pltpu.make_async_remote_copy(
            src_ref=every.at[origin, half],
            dst_ref=every.at[origin, half],
            send_sem=pass_send.at[send],
            recv_sem=pass_recv.at[origin, half],
            device_id={"col": to},
            device_id_type=MESH,
        )

    def unpack(origin, half):
        where[pl.ds(2 * origin + half, 1), :] = every[origin, half, 128:129, :]
        for i in range(2):
            word = every[origin, half, 64 * i : 64 * i + 64, :]
            y, x = word >> 16, (word << 16) >> 16
            at = pl.ds(pl.multiple_of(origin * share + half * 128 + 64 * i, 64), 64)
            parts[at, :] = jnp.concatenate(bytes_of(y) + bytes_of(x), 1)

    lax.fori_loop(0, 32, arrive, 0)
    gather(0)
    sends = [handed(col, 0, right, 0), handed(col, 0, left, 1)]
    sends[0].start()
    sends[1].start()
    unpack(col, 0)
    lax.fori_loop(32, pieces - 1, arrive, 0)
    gather(1)
    sends += [handed(col, 1, left, 2), handed(col, 1, right, 3)]
    sends[2].start()
    sends[3].start()
    up.start()
    down.start()
    handed(left, 0, left, 0).wait_recv()
    sends.append(handed(left, 0, right, 4))
    sends[4].start()
    unpack(col, 1)
    unpack(left, 0)
    handed(right, 0, right, 0).wait_recv()
    unpack(right, 0)
    handed(right, 1, right, 0).wait_recv()
    sends.append(handed(right, 1, left, 5))
    sends[5].start()
    unpack(right, 1)
    handed(left, 1, left, 0).wait_recv()
    unpack(left, 1)
    handed(far, 0, left, 0).wait_recv()
    unpack(far, 0)
    handed(far, 1, right, 0).wait_recv()
    unpack(far, 1)

    def settle(i, _):
        base = i * 512
        words[pl.ds(pl.multiple_of(base, 512), 512), :] = joined(
            jnp.dot(one_hot(base, 512), parts[...], preferred_element_type=f32)
        )
        return 0

    lax.fori_loop(0, 2, settle, 0)
    place_dep.wait()
    step_of = transport(dep, words, spread, cells, fact_y, fact_x, floors)
    steps = blocks // STEP
    side = steps // 4

    lax.fori_loop(side, steps - side, step_of, 0)
    quarter = cells.shape[0] // 4

    def leave(first, count, i):
        at = pl.ds(first * quarter, count * quarter)
        return pltpu.make_async_copy(cells.at[at], out.at[at], out_sem.at[i])

    leave(1, 2, 0).start()
    up.wait()
    widen(low, 0)
    down.wait()
    widen(high, (edge + tracers.shape[0]) // 32)

    def outer(i, _):
        return step_of(i + (i // side) * (steps // 2), 0)

    lax.fori_loop(0, 2 * side, outer, 0)
    leave(0, 1, 1).start()
    leave(3, 1, 2).start()

    def sent(turn, _):
        message(turn).wait_send()
        return 0

    lax.fori_loop(0, pieces - 1, sent, 0)
    for copy in sends:
        copy.wait_send()
    leave(1, 2, 0).wait()
    leave(0, 1, 1).wait()
    leave(3, 1, 2).wait()


def hand_out(whole, out, held, in_sem, out_sem):
    piece = out.shape[0] // 4
    at = [pl.ds(i * piece, piece) for i in range(4)]
    entering = [pltpu.make_async_copy(whole.at[p], held.at[p], in_sem.at[i]) for i, p in enumerate(at)]
    leaving = [pltpu.make_async_copy(held.at[p], out.at[p], out_sem.at[i]) for i, p in enumerate(at)]
    for copy in entering:
        copy.start()
    for first, second in zip(entering, leaving):
        first.wait()
        second.start()
    for copy in leaving:
        copy.wait()


def clear_factors(fact_y, fact_x):
    def clear(i, _):
        at = pl.ds(pl.multiple_of(i * 512, 512), 512)
        fact_y[at, :] = jnp.zeros((512, 128), f32)
        fact_x[at, :] = jnp.zeros((512, 128), f32)
        return 0

    lax.fori_loop(0, fact_y.shape[0] // 512, clear, 0)


def lagrange(t):
    a, b, c = t + 1.0, t - 1.0, t - 2.0
    tb, ac = t * b, a * c
    return tb * c * (-1.0 / 6.0), ac * b * 0.5, ac * t * (-0.5), a * tb * (1.0 / 6.0)


def rows_at(x, index):
    return jnp.take_along_axis(x, index, axis=0, mode="promise_in_bounds")


def folded(a, b, d):
    sub = iota((8, 128), 0)
    mine = (sub & d) == 0
    kept, moved = jnp.where(mine, a, b), jnp.where(mine, b, a)
    return kept + rows_at(moved, sub ^ d)


def transport(dep, words, spread, out, fact_y, fact_x, floors):
    blocks = words.shape[0]
    cell_row = iota((8, 128), 1) >> 4
    cell_col = iota((8, 128), 1) & 15
    sub = iota((8, 128), 0)
    zero = jnp.zeros((8, 128), f32)

    def factors(i, _):
        for u in range(4):
            g = i * 4 + u
            at = pl.ds(pl.multiple_of(g * 8, 8), 8)
            word = words[at, :]
            pos_y = (cell_row + 8) * UNIT - (word >> 16)
            pos_x = cell_col * UNIT - ((word << 16) >> 16)
            wy = lagrange((pos_y & (UNIT - 1)).astype(f32) * (1.0 / UNIT))
            wx = lagrange((pos_x & (UNIT - 1)).astype(f32) * (1.0 / UNIT))
            for p in range(4):
                fact_y[pl.ds(g * 64 + p, 8, stride=8), :] = wy[p]
                fact_x[pl.ds(g * 64 + p, 8, stride=8), :] = wx[p]
            floors[0, at, :] = pos_y >> 12
            floors[1, at, :] = pos_x >> 12
        return 0

    lax.fori_loop(0, blocks // 32, factors, 0)

    def two_blocks(first):
        prods = []
        for e in (0, 1):
            b = first + e
            lines = []
            for k in range(3):
                lines.append(spread[dep[k, b]])
            uy = (sub + 1) - jnp.broadcast_to(floors[0, pl.ds(b, 1), :], (8, 128))
            ux = (sub + 1) - jnp.broadcast_to(floors[1, pl.ds(b, 1), :], (8, 128))
            at = pl.ds(pl.multiple_of(b * 8, 8), 8)
            gy = rows_at(fact_y[at, :], uy & 7)
            gx = rows_at(fact_x[at, :], ux & 7)
            near = (ux & 8) == 0
            cols = jnp.concatenate([jnp.where(near, gx, zero), jnp.where(near, zero, gx)], 0).astype(bf16)
            sums = jnp.dot(
                jnp.concatenate(lines, 0), jnp.concatenate([cols] * 8, 0), preferred_element_type=f32
            )
            in0, in1 = uy >= 0, uy >= -8
            for t in range(4):
                r0, r1, r2 = (sums[32 * k + 8 * t : 32 * k + 8 * t + 8] for k in range(3))
                prods.append(jnp.where(in0, r0, jnp.where(in1, r1, r2)) * gy)
        for d in (4, 2, 1):
            prods = [folded(prods[i], prods[i + d], d) for i in range(d)]
        return prods[0]

    def some(i, _):
        for q in range(0, STEP, 4):
            b = i * STEP + q
            four = jnp.concatenate([two_blocks(b), two_blocks(b + 2)], 0).astype(bf16)
            out[pl.ds(pl.multiple_of(b * 4, 16), 16), :] = four
        return 0

    return some


def on_device(tracers, winds, tile_owner, departure):
    pieces = lax.axis_size(AXES)
    blocks = tile_owner.shape[0]
    panel = tracers.shape[0]
    edge = blocks // 4 * panel
    lines = tracers.reshape(panel, blocks, 128).transpose(1, 0, 2).reshape(blocks * panel, 128)
    wind_lines = winds.reshape(2, blocks, 128).transpose(1, 0, 2).reshape(blocks * 2, 128)
    dma = pltpu.SemaphoreType.DMA
    out = pl.pallas_call(
        advect,
        out_shape=jax.ShapeDtypeStruct((blocks * panel, 128), bf16),
        in_specs=[pl.BlockSpec(memory_space=pltpu.HBM)] * 4,
        out_specs=pl.BlockSpec(memory_space=pltpu.HBM),
        scratch_shapes=[
            pltpu.VMEM((blocks * 2, 128), f32),
            pltpu.VMEM((blocks // 128, 128), i32),
            pltpu.VMEM((blocks * panel, 128), bf16),
            pltpu.SMEM((3, blocks), i32),
            pltpu.VMEM((edge, 128), bf16),
            pltpu.VMEM((edge, 128), bf16),
            pltpu.VMEM((blocks, 512), bf16),
            pltpu.VMEM((pieces, 8, 128), i32),
            pltpu.VMEM((pieces, 8, 128), i32),
            pltpu.VMEM((4, 2, 136, 128), i32),
            pltpu.VMEM((8, 128), i32),
            pltpu.VMEM((blocks, 128), i32),
            pltpu.VMEM((blocks * 3 // 2, 32, 128), bf16),
            pltpu.VMEM((blocks * 8, 128), f32),
            pltpu.VMEM((blocks * 8, 128), f32),
            pltpu.VMEM((2, blocks, 128), i32),
            pltpu.VMEM((3, blocks), i32),
            pltpu.VMEM((3, blocks), i32),
            pltpu.VMEM((blocks * panel, 128), bf16),
            dma((3,)),
            dma((pieces,)),
            dma((pieces,)),
            dma((2,)),
            dma((2,)),
            dma((6,)),
            dma((4, 2)),
            dma((5,)),
        ],
        compiler_params=pltpu.CompilerParams(
            collective_id=0, has_side_effects=True, vmem_limit_bytes=60 << 20
        ),
    )(wind_lines, tile_owner.reshape(blocks // 128, 128), lines, departure.T)
    out = pl.pallas_call(
        hand_out,
        out_shape=jax.ShapeDtypeStruct(out.shape, bf16),
        in_specs=[pl.BlockSpec(memory_space=pltpu.HBM)],
        out_specs=pl.BlockSpec(memory_space=pltpu.HBM),
        scratch_shapes=[pltpu.VMEM(out.shape, bf16), dma((4,)), dma((4,))],
        compiler_params=pltpu.CompilerParams(vmem_limit_bytes=60 << 20),
    )(out)
    return out.reshape(blocks, panel, 128).transpose(1, 0, 2).reshape(panel, blocks * 128)


def solution(mesh):
    placed = (
        P("col", AXES),
        P(None, AXES),
        P(AXES),
        P(AXES, None),
    )
    return jax.shard_map(
        on_device, mesh=mesh, in_specs=placed, out_specs=P("col", AXES), check_vma=False
    )
```

```python
import functools

import jax
import jax.numpy as jnp
from jax import lax
from jax.experimental import pallas as pl
from jax.experimental.pallas import tpu as pltpu
from jax.sharding import PartitionSpec as P

f32, i32, bf16 = jnp.float32, jnp.int32, jnp.bfloat16
AXES = ("row", "rep")
MESH = pl.DeviceIdType.MESH
ROWS = 5
UNIT = 4096
STEP = 256


def iota(shape, dim):
    return lax.broadcasted_iota(i32, shape, dim)


def pick(cond):
    return jnp.where(cond, 1.0, 0.0).astype(bf16)


def bytes_of(code):
    return (code >> 8).astype(f32).astype(bf16), (code & 255).astype(f32).astype(bf16)


def joined(parts):
    y = (parts[:, 0:128] * 256.0 + parts[:, 128:256]).astype(i32)
    x = (parts[:, 256:384] * 256.0 + parts[:, 384:512]).astype(i32)
    return (y << 16) | (x & 65535)


def place_of(piece):
    return {"row": piece // 2, "rep": piece % 2}


def advect(
    winds_hbm, owner_hbm, tracers_hbm, dep_hbm, out,
    winds, owner, tracers, dep, low, high, parts, snd, rcv, every, where,
    words, spread, fact_y, fact_x, floors, dep_far, dep_near, cells, out_sem,
    send_sem, recv_sem, halo_send, halo_recv, pass_send, pass_recv, load_sem,
):
    pieces = snd.shape[0]
    blocks = words.shape[0]
    edge = low.shape[0]
    share = blocks // 4
    me = lax.axis_index(AXES)
    col = lax.axis_index("col")
    after = lax.rem(me + 1, pieces)
    before = lax.rem(me + pieces - 1, pieces)

    barrier = pltpu.get_barrier_semaphore()

    def greet(i, _):
        to = lax.rem(me + i, pieces)
        pl.semaphore_signal(barrier, inc=1, device_id=place_of(to), device_id_type=MESH)
        return 0

    lax.fori_loop(1, pieces, greet, 0)
    left, right = lax.rem(col + 3, 4), lax.rem(col + 1, 4)
    for c in (left, right):
        pl.semaphore_signal(barrier, inc=1, device_id={"col": c}, device_id_type=MESH)

    load_owner = pltpu.make_async_copy(owner_hbm, owner, load_sem.at[0])
    load_winds = pltpu.make_async_copy(winds_hbm, winds, load_sem.at[1])
    load_tracers = pltpu.make_async_copy(tracers_hbm, tracers, load_sem.at[2])
    load_owner.start()
    load_winds.start()
    load_tracers.start()
    load_dep = pltpu.make_async_copy(dep_hbm, dep_far, load_sem.at[3])
    load_dep.start()

    load_owner.wait()
    lanes = iota((128, 128), 1)
    step = jnp.concatenate([pick(iota((128, 128), 0) < lanes), jnp.ones((128, 128), bf16)], 1)
    run = jnp.zeros((pieces, 128), f32)
    sums = jnp.zeros((pieces, 128), f32)
    for g in range(blocks // 128):
        own = owner[g : g + 1, :]
        to = own // blocks
        slot = own - to * blocks
        mine = iota((pieces, 128), 0) == to
        hot = pick(mine)
        seen = jnp.dot(hot, step, preferred_element_type=f32)
        rank = jnp.sum(jnp.where(mine, seen[:, :128] + run, 0.0), axis=0, keepdims=True)
        rank = rank.astype(i32) - 4 * col
        run = run + seen[:, 128:]
        here = (rank >= 0) & (rank < 4)
        where[g : g + 1, :] = jnp.where(here, to * 4 + rank, -1)
        ahead = jnp.where(to >= me, to - me, to - me + pieces)
        turn = ahead - 1 - pieces // 4
        turn = jnp.where(turn < 0, turn + pieces - 1, turn)
        turn = jnp.where(ahead == 0, pieces - 1, turn)
        lane = iota((128, 128), 0) == jnp.where(here, rank + 4 * (turn & 31), -1)
        for part, scale in ((slot >> 5, 32.0), (slot & 31, 1.0)):
            spot = jnp.where(lane, part.astype(f32), 0.0).astype(bf16)
            sums = sums + scale * lax.dot_general(
                hot, spot, (((1,), (1,)), ((), ())), preferred_element_type=f32
            )
    for d in range(pieces):
        snd[d, 4:5, :] = sums[d : d + 1].astype(i32)

    load_winds.wait()

    def encode(i, _):
        base = i * 64
        y = jnp.concatenate([winds[pl.ds((base + 8 * j) * 2, 8, stride=2), :] for j in range(8)], 0)
        x = jnp.concatenate([winds[pl.ds((base + 8 * j) * 2 + 1, 8, stride=2), :] for j in range(8)], 0)
        cy = jnp.round(jnp.tanh(y) * (6.0 * UNIT)).astype(i32)
        cx = jnp.round(jnp.tanh(x) * (4.0 * UNIT)).astype(i32)
        parts[pl.ds(pl.multiple_of(base, 64), 64), :] = jnp.concatenate(bytes_of(cy) + bytes_of(cx), 1)
        return 0

    lax.fori_loop(0, blocks // 64, encode, 0)

    def one_hot(base, height):
        return jnp.concatenate(
            [pick(iota((height, 128), 0) + base == where[g : g + 1, :]) for g in range(blocks // 128)], 1
        )

    word = joined(jnp.dot(one_hot(0, share), parts[...], preferred_element_type=f32))
    snd[:, 0:4, :] = word.reshape(pieces, 4, 128)

    pl.semaphore_wait(barrier, pieces + 1)

    def message(turn):
        to = lax.rem(me + 1 + lax.rem(turn + pieces // 4, pieces - 1), pieces)
        return pltpu.make_async_remote_copy(
            src_ref=snd.at[to, pl.ds(0, ROWS)],
            dst_ref=rcv.at[turn, pl.ds(0, ROWS)],
            send_sem=send_sem.at[turn],
            recv_sem=recv_sem.at[turn],
            device_id=place_of(to),
            device_id_type=MESH,
        )

    def start(turn, _):
        message(turn).start()
        return 0

    lax.fori_loop(0, pieces - 1, start, 0)

    up = pltpu.make_async_remote_copy(
        src_ref=tracers_hbm.at[pl.ds(tracers.shape[0] - edge, edge)],
        dst_ref=low,
        send_sem=halo_send.at[0],
        recv_sem=halo_recv.at[0],
        device_id=place_of(after),
        device_id_type=MESH,
    )
    down = pltpu.make_async_remote_copy(
        src_ref=tracers_hbm.at[pl.ds(0, edge)],
        dst_ref=high,
        send_sem=halo_send.at[1],
        recv_sem=halo_recv.at[1],
        device_id=place_of(before),
        device_id_type=MESH,
    )
    rcv[pieces - 1, 0:ROWS, :] = snd[me, 0:ROWS, :]

    own_row = (iota((8, 128), 1) >> 4) == iota((8, 128), 0)

    def widen(ref, first):
        def one(i, _):
            x = ref[pl.ds(pl.multiple_of(i * 32, 32), 32), :].astype(f32)
            y = jnp.where(own_row[None], jnp.broadcast_to(x[:, None, :], (32, 8, 128)), 0.0)
            spread[pl.ds((first + i) * 8, 8)] = y.reshape(8, 32, 128).astype(bf16)
            return 0

        lax.fori_loop(0, ref.shape[0] // 32, one, 0)

    load_tracers.wait()
    widen(tracers, edge // 32)
    clear_factors(fact_y, fact_x)

    load_dep.wait()
    reach = blocks // 4
    ahead = dep_far[...] - (me * blocks - reach)
    total = blocks * pieces
    ahead = jnp.where(ahead < 0, ahead + total, jnp.where(ahead >= total, ahead - total, ahead))
    dep_near[...] = jnp.clip(ahead, 0, blocks + 2 * reach - 1)
    place_dep = pltpu.make_async_copy(dep_near, dep, load_sem.at[4])
    place_dep.start()

    def arrive(turn, _):
        message(turn).wait_recv()
        return 0

    far = lax.rem(col + 2, 4)

    def gather(half):
        at = pl.ds(32 * half, 32)
        every[col, half, 0:128, :] = rcv[at, 0:4, :].reshape(128, 128)
        rows = [rcv[32 * half + s, 4:5, :] for s in range(32)]
        every[col, half, 128:129, :] = functools.reduce(jnp.add, rows)

    def handed(origin, half, to, send):
        return pltpu.make_async_remote_copy(
            src_ref=every.at[origin, half],
            dst_ref=every.at[origin, half],
            send_sem=pass_send.at[send],
            recv_sem=pass_recv.at[origin, half],
            device_id={"col": to},
            device_id_type=MESH,
        )

    def unpack(origin, half):
        where[pl.ds(2 * origin + half, 1), :] = every[origin, half, 128:129, :]
        for i in range(2):
            word = every[origin, half, 64 * i : 64 * i + 64, :]
            y, x = word >> 16, (word << 16) >> 16
            at = pl.ds(pl.multiple_of(origin * share + half * 128 + 64 * i, 64), 64)
            parts[at, :] = jnp.concatenate(bytes_of(y) + bytes_of(x), 1)

    lax.fori_loop(0, 32, arrive, 0)
    gather(0)
    sends = [handed(col, 0, right, 0), handed(col, 0, left, 1)]
    sends[0].start()
    sends[1].start()
    unpack(col, 0)
    lax.fori_loop(32, pieces - 1, arrive, 0)
    gather(1)
    sends += [handed(col, 1, left, 2), handed(col, 1, right, 3)]
    sends[2].start()
    sends[3].start()
    up.start()
    down.start()
    handed(left, 0, left, 0).wait_recv()
    sends.append(handed(left, 0, right, 4))
    sends[4].start()
    unpack(col, 1)
    unpack(left, 0)
    handed(right, 0, right, 0).wait_recv()
    unpack(right, 0)
    handed(right, 1, right, 0).wait_recv()
    sends.append(handed(right, 1, left, 5))
    sends[5].start()
    unpack(right, 1)
    handed(left, 1, left, 0).wait_recv()
    unpack(left, 1)
    handed(far, 0, left, 0).wait_recv()
    unpack(far, 0)
    handed(far, 1, right, 0).wait_recv()
    unpack(far, 1)

    def settle(i, _):
        base = i * 512
        words[pl.ds(pl.multiple_of(base, 512), 512), :] = joined(
            jnp.dot(one_hot(base, 512), parts[...], preferred_element_type=f32)
        )
        return 0

    lax.fori_loop(0, 2, settle, 0)
    place_dep.wait()
    step_of = transport(dep, words, spread, cells, fact_y, fact_x, floors)
    quarter = cells.shape[0] // 4

    def leave(first, count, i):
        at = pl.ds(first * quarter, count * quarter)
        return pltpu.make_async_copy(cells.at[at], out.at[at], out_sem.at[i])

    def quarters(i, _):
        @pl.when(i == 2)
        def _():
            leave(1, 2, 0).start()
            up.wait()
            widen(low, 0)
            down.wait()
            widen(high, (edge + tracers.shape[0]) // 32)

        return step_of(lax.rem(i + 1, 3) + 2 * (i // 3), 0)

    lax.fori_loop(0, blocks // STEP, quarters, 0)
    leave(0, 1, 1).start()
    leave(3, 1, 2).start()

    def sent(turn, _):
        message(turn).wait_send()
        return 0

    lax.fori_loop(0, pieces - 1, sent, 0)
    for copy in sends:
        copy.wait_send()
    leave(1, 2, 0).wait()
    leave(0, 1, 1).wait()
    leave(3, 1, 2).wait()


def hand_out(whole, out, held, in_sem, out_sem):
    piece = out.shape[0] // 4
    at = [pl.ds(i * piece, piece) for i in range(4)]
    entering = [pltpu.make_async_copy(whole.at[p], held.at[p], in_sem.at[i]) for i, p in enumerate(at)]
    leaving = [pltpu.make_async_copy(held.at[p], out.at[p], out_sem.at[i]) for i, p in enumerate(at)]
    for copy in entering:
        copy.start()
    for first, second in zip(entering, leaving):
        first.wait()
        second.start()
    for copy in leaving:
        copy.wait()


def clear_factors(fact_y, fact_x):
    def clear(i, _):
        at = pl.ds(pl.multiple_of(i * 512, 512), 512)
        fact_y[at, :] = jnp.zeros((512, 128), f32)
        fact_x[at, :] = jnp.zeros((512, 128), f32)
        return 0

    lax.fori_loop(0, fact_y.shape[0] // 512, clear, 0)


def lagrange(t):
    a, b, c = t + 1.0, t - 1.0, t - 2.0
    tb, ac = t * b, a * c
    return tb * c * (-1.0 / 6.0), ac * b * 0.5, ac * t * (-0.5), a * tb * (1.0 / 6.0)


def rows_at(x, index):
    return jnp.take_along_axis(x, index, axis=0, mode="promise_in_bounds")


def folded(a, b, d):
    sub = iota((8, 128), 0)
    mine = (sub & d) == 0
    kept, moved = jnp.where(mine, a, b), jnp.where(mine, b, a)
    return kept + rows_at(moved, sub ^ d)


def transport(dep, words, spread, out, fact_y, fact_x, floors):
    blocks = words.shape[0]
    cell_row = iota((8, 128), 1) >> 4
    cell_col = iota((8, 128), 1) & 15
    sub = iota((8, 128), 0)
    zero = jnp.zeros((8, 128), f32)

    def factors(i, _):
        for u in range(4):
            g = i * 4 + u
            at = pl.ds(pl.multiple_of(g * 8, 8), 8)
            word = words[at, :]
            pos_y = (cell_row + 8) * UNIT - (word >> 16)
            pos_x = cell_col * UNIT - ((word << 16) >> 16)
            wy = lagrange((pos_y & (UNIT - 1)).astype(f32) * (1.0 / UNIT))
            wx = lagrange((pos_x & (UNIT - 1)).astype(f32) * (1.0 / UNIT))
            for p in range(4):
                fact_y[pl.ds(g * 64 + p, 8, stride=8), :] = wy[p]
                fact_x[pl.ds(g * 64 + p, 8, stride=8), :] = wx[p]
            floors[0, at, :] = pos_y >> 12
            floors[1, at, :] = pos_x >> 12
        return 0

    lax.fori_loop(0, blocks // 32, factors, 0)

    def two_blocks(first):
        prods = []
        for e in (0, 1):
            b = first + e
            lines = []
            for k in range(3):
                lines.append(spread[dep[k, b]])
            uy = (sub + 1) - jnp.broadcast_to(floors[0, pl.ds(b, 1), :], (8, 128))
            ux = (sub + 1) - jnp.broadcast_to(floors[1, pl.ds(b, 1), :], (8, 128))
            at = pl.ds(pl.multiple_of(b * 8, 8), 8)
            gy = rows_at(fact_y[at, :], uy & 7)
            gx = rows_at(fact_x[at, :], ux & 7)
            near = (ux & 8) == 0
            cols = jnp.concatenate([jnp.where(near, gx, zero), jnp.where(near, zero, gx)], 0).astype(bf16)
            sums = jnp.dot(
                jnp.concatenate(lines, 0), jnp.concatenate([cols] * 8, 0), preferred_element_type=f32
            )
            in0, in1 = uy >= 0, uy >= -8
            for t in range(4):
                r0, r1, r2 = (sums[32 * k + 8 * t : 32 * k + 8 * t + 8] for k in range(3))
                prods.append(jnp.where(in0, r0, jnp.where(in1, r1, r2)) * gy)
        for d in (4, 2, 1):
            prods = [folded(prods[i], prods[i + d], d) for i in range(d)]
        return prods[0]

    def some(i, _):
        for q in range(0, STEP, 4):
            b = i * STEP + q
            four = jnp.concatenate([two_blocks(b), two_blocks(b + 2)], 0).astype(bf16)
            out[pl.ds(pl.multiple_of(b * 4, 16), 16), :] = four
        return 0

    return some


def on_device(tracers, winds, tile_owner, departure):
    pieces = lax.axis_size(AXES)
    blocks = tile_owner.shape[0]
    panel = tracers.shape[0]
    edge = blocks // 4 * panel
    lines = tracers.reshape(panel, blocks, 128).transpose(1, 0, 2).reshape(blocks * panel, 128)
    wind_lines = winds.reshape(2, blocks, 128).transpose(1, 0, 2).reshape(blocks * 2, 128)
    dma = pltpu.SemaphoreType.DMA
    out = pl.pallas_call(
        advect,
        out_shape=jax.ShapeDtypeStruct((blocks * panel, 128), bf16),
        in_specs=[pl.BlockSpec(memory_space=pltpu.HBM)] * 4,
        out_specs=pl.BlockSpec(memory_space=pltpu.HBM),
        scratch_shapes=[
            pltpu.VMEM((blocks * 2, 128), f32),
            pltpu.VMEM((blocks // 128, 128), i32),
            pltpu.VMEM((blocks * panel, 128), bf16),
            pltpu.SMEM((3, blocks), i32),
            pltpu.VMEM((edge, 128), bf16),
            pltpu.VMEM((edge, 128), bf16),
            pltpu.VMEM((blocks, 512), bf16),
            pltpu.VMEM((pieces, 8, 128), i32),
            pltpu.VMEM((pieces, 8, 128), i32),
            pltpu.VMEM((4, 2, 136, 128), i32),
            pltpu.VMEM((8, 128), i32),
            pltpu.VMEM((blocks, 128), i32),
            pltpu.VMEM((blocks * 3 // 2, 32, 128), bf16),
            pltpu.VMEM((blocks * 8, 128), f32),
            pltpu.VMEM((blocks * 8, 128), f32),
            pltpu.VMEM((2, blocks, 128), i32),
            pltpu.VMEM((3, blocks), i32),
            pltpu.VMEM((3, blocks), i32),
            pltpu.VMEM((blocks * panel, 128), bf16),
            dma((3,)),
            dma((pieces,)),
            dma((pieces,)),
            dma((2,)),
            dma((2,)),
            dma((6,)),
            dma((4, 2)),
            dma((5,)),
        ],
        compiler_params=pltpu.CompilerParams(
            collective_id=0, has_side_effects=True, vmem_limit_bytes=60 << 20
        ),
    )(wind_lines, tile_owner.reshape(blocks // 128, 128), lines, departure.T)
    out = pl.pallas_call(
        hand_out,
        out_shape=jax.ShapeDtypeStruct(out.shape, bf16),
        in_specs=[pl.BlockSpec(memory_space=pltpu.HBM)],
        out_specs=pl.BlockSpec(memory_space=pltpu.HBM),
        scratch_shapes=[pltpu.VMEM(out.shape, bf16), dma((4,)), dma((4,))],
        compiler_params=pltpu.CompilerParams(vmem_limit_bytes=60 << 20),
    )(out)
    return out.reshape(blocks, panel, 128).transpose(1, 0, 2).reshape(panel, blocks * 128)


def solution(mesh):
    placed = (
        P("col", AXES),
        P(None, AXES),
        P(AXES),
        P(AXES, None),
    )
    return jax.shard_map(
        on_device, mesh=mesh, in_specs=placed, out_specs=P("col", AXES), check_vma=False
    )
```

```python
import functools

import jax
import jax.numpy as jnp
from jax import lax
from jax.experimental import pallas as pl
from jax.experimental.pallas import tpu as pltpu
from jax.sharding import PartitionSpec as P

f32, i32, bf16 = jnp.float32, jnp.int32, jnp.bfloat16
AXES = ("row", "rep")
MESH = pl.DeviceIdType.MESH
ROWS = 5
UNIT = 4096
STEP = 256


def iota(shape, dim):
    return lax.broadcasted_iota(i32, shape, dim)


def pick(cond):
    return jnp.where(cond, 1.0, 0.0).astype(bf16)


def bytes_of(code):
    return (code >> 8).astype(f32).astype(bf16), (code & 255).astype(f32).astype(bf16)


def joined(parts):
    y = (parts[:, 0:128] * 256.0 + parts[:, 128:256]).astype(i32)
    x = (parts[:, 256:384] * 256.0 + parts[:, 384:512]).astype(i32)
    return (y << 16) | (x & 65535)


def place_of(piece):
    return {"row": piece // 2, "rep": piece % 2}


def advect(
    winds_hbm, owner_hbm, tracers_hbm, dep_hbm, out,
    winds, owner, tracers, dep, low, high, parts, snd, rcv, every, where,
    words, spread, fact_y, fact_x, floors, dep_far, dep_near, cells, out_sem,
    send_sem, recv_sem, halo_send, halo_recv, pass_send, pass_recv, load_sem,
):
    pieces = snd.shape[0]
    blocks = words.shape[0]
    edge = low.shape[0]
    share = blocks // 4
    me = lax.axis_index(AXES)
    col = lax.axis_index("col")
    after = lax.rem(me + 1, pieces)
    before = lax.rem(me + pieces - 1, pieces)

    barrier = pltpu.get_barrier_semaphore()

    def greet(i, _):
        to = lax.rem(me + i, pieces)
        pl.semaphore_signal(barrier, inc=1, device_id=place_of(to), device_id_type=MESH)
        return 0

    lax.fori_loop(1, pieces, greet, 0)
    left, right = lax.rem(col + 3, 4), lax.rem(col + 1, 4)
    for c in (left, right):
        pl.semaphore_signal(barrier, inc=1, device_id={"col": c}, device_id_type=MESH)

    load_owner = pltpu.make_async_copy(owner_hbm, owner, load_sem.at[0])
    load_winds = pltpu.make_async_copy(winds_hbm, winds, load_sem.at[1])
    load_tracers = pltpu.make_async_copy(tracers_hbm, tracers, load_sem.at[2])
    load_owner.start()
    load_winds.start()
    load_tracers.start()
    load_dep = pltpu.make_async_copy(dep_hbm, dep_far, load_sem.at[3])
    load_dep.start()

    load_owner.wait()
    lanes = iota((128, 128), 1)
    step = jnp.concatenate([pick(iota((128, 128), 0) < lanes), jnp.ones((128, 128), bf16)], 1)
    run = jnp.zeros((pieces, 128), f32)
    sums = jnp.zeros((pieces, 128), f32)
    for g in range(blocks // 128):
        own = owner[g : g + 1, :]
        to = own // blocks
        slot = own - to * blocks
        mine = iota((pieces, 128), 0) == to
        hot = pick(mine)
        seen = jnp.dot(hot, step, preferred_element_type=f32)
        rank = jnp.sum(jnp.where(mine, seen[:, :128] + run, 0.0), axis=0, keepdims=True)
        rank = rank.astype(i32) - 4 * col
        run = run + seen[:, 128:]
        here = (rank >= 0) & (rank < 4)
        where[g : g + 1, :] = jnp.where(here, to * 4 + rank, -1)
        ahead = jnp.where(to >= me, to - me, to - me + pieces)
        turn = jnp.where(ahead >= pieces // 2, 2 * ahead - pieces, pieces - 1 - 2 * ahead)
        lane = iota((128, 128), 0) == jnp.where(here, rank + 4 * (turn & 31), -1)
        for part, scale in ((slot >> 5, 32.0), (slot & 31, 1.0)):
            spot = jnp.where(lane, part.astype(f32), 0.0).astype(bf16)
            sums = sums + scale * lax.dot_general(
                hot, spot, (((1,), (1,)), ((), ())), preferred_element_type=f32
            )
    for d in range(pieces):
        snd[d, 4:5, :] = sums[d : d + 1].astype(i32)

    load_winds.wait()

    def encode(i, _):
        base = i * 64
        y = jnp.concatenate([winds[pl.ds((base + 8 * j) * 2, 8, stride=2), :] for j in range(8)], 0)
        x = jnp.concatenate([winds[pl.ds((base + 8 * j) * 2 + 1, 8, stride=2), :] for j in range(8)], 0)
        cy = jnp.round(jnp.tanh(y) * (6.0 * UNIT)).astype(i32)
        cx = jnp.round(jnp.tanh(x) * (4.0 * UNIT)).astype(i32)
        parts[pl.ds(pl.multiple_of(base, 64), 64), :] = jnp.concatenate(bytes_of(cy) + bytes_of(cx), 1)
        return 0

    lax.fori_loop(0, blocks // 64, encode, 0)

    def one_hot(base, height):
        return jnp.concatenate(
            [pick(iota((height, 128), 0) + base == where[g : g + 1, :]) for g in range(blocks // 128)], 1
        )

    word = joined(jnp.dot(one_hot(0, share), parts[...], preferred_element_type=f32))
    snd[:, 0:4, :] = word.reshape(pieces, 4, 128)

    pl.semaphore_wait(barrier, pieces + 1)

    def message(turn):
        half = (turn + 1) // 2
        to = lax.rem(me + pieces // 2 + half - 2 * half * lax.rem(turn, 2), pieces)
        return pltpu.make_async_remote_copy(
            src_ref=snd.at[to, pl.ds(0, ROWS)],
            dst_ref=rcv.at[turn, pl.ds(0, ROWS)],
            send_sem=send_sem.at[turn],
            recv_sem=recv_sem.at[turn],
            device_id=place_of(to),
            device_id_type=MESH,
        )

    def start(turn, _):
        message(turn).start()
        return 0

    lax.fori_loop(0, pieces - 1, start, 0)

    up = pltpu.make_async_remote_copy(
        src_ref=tracers_hbm.at[pl.ds(tracers.shape[0] - edge, edge)],
        dst_ref=low,
        send_sem=halo_send.at[0],
        recv_sem=halo_recv.at[0],
        device_id=place_of(after),
        device_id_type=MESH,
    )
    down = pltpu.make_async_remote_copy(
        src_ref=tracers_hbm.at[pl.ds(0, edge)],
        dst_ref=high,
        send_sem=halo_send.at[1],
        recv_sem=halo_recv.at[1],
        device_id=place_of(before),
        device_id_type=MESH,
    )
    rcv[pieces - 1, 0:ROWS, :] = snd[me, 0:ROWS, :]

    own_row = (iota((8, 128), 1) >> 4) == iota((8, 128), 0)

    def widen(ref, first):
        def one(i, _):
            x = ref[pl.ds(pl.multiple_of(i * 32, 32), 32), :].astype(f32)
            y = jnp.where(own_row[None], jnp.broadcast_to(x[:, None, :], (32, 8, 128)), 0.0)
            spread[pl.ds((first + i) * 8, 8)] = y.reshape(8, 32, 128).astype(bf16)
            return 0

        lax.fori_loop(0, ref.shape[0] // 32, one, 0)

    load_tracers.wait()
    widen(tracers, edge // 32)
    clear_factors(fact_y, fact_x)

    load_dep.wait()
    reach = blocks // 4
    ahead = dep_far[...] - (me * blocks - reach)
    total = blocks * pieces
    ahead = jnp.where(ahead < 0, ahead + total, jnp.where(ahead >= total, ahead - total, ahead))
    dep_near[...] = jnp.clip(ahead, 0, blocks + 2 * reach - 1)
    place_dep = pltpu.make_async_copy(dep_near, dep, load_sem.at[4])
    place_dep.start()

    def arrive(turn, _):
        message(turn).wait_recv()
        return 0

    far = lax.rem(col + 2, 4)

    def gather(half):
        at = pl.ds(32 * half, 32)
        every[col, half, 0:128, :] = rcv[at, 0:4, :].reshape(128, 128)
        rows = [rcv[32 * half + s, 4:5, :] for s in range(32)]
        every[col, half, 128:129, :] = functools.reduce(jnp.add, rows)

    def handed(origin, half, to, send):
        return pltpu.make_async_remote_copy(
            src_ref=every.at[origin, half],
            dst_ref=every.at[origin, half],
            send_sem=pass_send.at[send],
            recv_sem=pass_recv.at[origin, half],
            device_id={"col": to},
            device_id_type=MESH,
        )

    def unpack(origin, half):
        where[pl.ds(2 * origin + half, 1), :] = every[origin, half, 128:129, :]
        for i in range(2):
            word = every[origin, half, 64 * i : 64 * i + 64, :]
            y, x = word >> 16, (word << 16) >> 16
            at = pl.ds(pl.multiple_of(origin * share + half * 128 + 64 * i, 64), 64)
            parts[at, :] = jnp.concatenate(bytes_of(y) + bytes_of(x), 1)

    lax.fori_loop(0, 32, arrive, 0)
    gather(0)
    sends = [handed(col, 0, right, 0), handed(col, 0, left, 1)]
    sends[0].start()
    sends[1].start()
    unpack(col, 0)
    lax.fori_loop(32, pieces - 1, arrive, 0)
    gather(1)
    sends += [handed(col, 1, left, 2), handed(col, 1, right, 3)]
    sends[2].start()
    sends[3].start()
    up.start()
    down.start()
    handed(left, 0, left, 0).wait_recv()
    sends.append(handed(left, 0, right, 4))
    sends[4].start()
    unpack(col, 1)
    unpack(left, 0)
    handed(right, 0, right, 0).wait_recv()
    unpack(right, 0)
    handed(right, 1, right, 0).wait_recv()
    sends.append(handed(right, 1, left, 5))
    sends[5].start()
    unpack(right, 1)
    handed(left, 1, left, 0).wait_recv()
    unpack(left, 1)
    handed(far, 0, left, 0).wait_recv()
    unpack(far, 0)
    handed(far, 1, right, 0).wait_recv()
    unpack(far, 1)

    def settle(i, _):
        base = i * 512
        words[pl.ds(pl.multiple_of(base, 512), 512), :] = joined(
            jnp.dot(one_hot(base, 512), parts[...], preferred_element_type=f32)
        )
        return 0

    lax.fori_loop(0, 2, settle, 0)
    place_dep.wait()
    step_of = transport(dep, words, spread, cells, fact_y, fact_x, floors)
    quarter = cells.shape[0] // 4

    def leave(first, count, i):
        at = pl.ds(first * quarter, count * quarter)
        return pltpu.make_async_copy(cells.at[at], out.at[at], out_sem.at[i])

    def quarters(i, _):
        @pl.when(i == 2)
        def _():
            leave(1, 2, 0).start()
            up.wait()
            widen(low, 0)
            down.wait()
            widen(high, (edge + tracers.shape[0]) // 32)

        return step_of(lax.rem(i + 1, 3) + 2 * (i // 3), 0)

    lax.fori_loop(0, blocks // STEP, quarters, 0)
    leave(0, 1, 1).start()
    leave(3, 1, 2).start()

    def sent(turn, _):
        message(turn).wait_send()
        return 0

    lax.fori_loop(0, pieces - 1, sent, 0)
    for copy in sends:
        copy.wait_send()
    leave(1, 2, 0).wait()
    leave(0, 1, 1).wait()
    leave(3, 1, 2).wait()


def hand_out(whole, out, held, in_sem, out_sem):
    piece = out.shape[0] // 4
    at = [pl.ds(i * piece, piece) for i in range(4)]
    entering = [pltpu.make_async_copy(whole.at[p], held.at[p], in_sem.at[i]) for i, p in enumerate(at)]
    leaving = [pltpu.make_async_copy(held.at[p], out.at[p], out_sem.at[i]) for i, p in enumerate(at)]
    for copy in entering:
        copy.start()
    for first, second in zip(entering, leaving):
        first.wait()
        second.start()
    for copy in leaving:
        copy.wait()


def clear_factors(fact_y, fact_x):
    def clear(i, _):
        at = pl.ds(pl.multiple_of(i * 512, 512), 512)
        fact_y[at, :] = jnp.zeros((512, 128), f32)
        fact_x[at, :] = jnp.zeros((512, 128), f32)
        return 0

    lax.fori_loop(0, fact_y.shape[0] // 512, clear, 0)


def lagrange(t):
    a, b, c = t + 1.0, t - 1.0, t - 2.0
    tb, ac = t * b, a * c
    return tb * c * (-1.0 / 6.0), ac * b * 0.5, ac * t * (-0.5), a * tb * (1.0 / 6.0)


def rows_at(x, index):
    return jnp.take_along_axis(x, index, axis=0, mode="promise_in_bounds")


def folded(a, b, d):
    sub = iota((8, 128), 0)
    mine = (sub & d) == 0
    kept, moved = jnp.where(mine, a, b), jnp.where(mine, b, a)
    return kept + rows_at(moved, sub ^ d)


def transport(dep, words, spread, out, fact_y, fact_x, floors):
    blocks = words.shape[0]
    cell_row = iota((8, 128), 1) >> 4
    cell_col = iota((8, 128), 1) & 15
    sub = iota((8, 128), 0)
    zero = jnp.zeros((8, 128), f32)

    def factors(i, _):
        for u in range(4):
            g = i * 4 + u
            at = pl.ds(pl.multiple_of(g * 8, 8), 8)
            word = words[at, :]
            pos_y = (cell_row + 8) * UNIT - (word >> 16)
            pos_x = cell_col * UNIT - ((word << 16) >> 16)
            wy = lagrange((pos_y & (UNIT - 1)).astype(f32) * (1.0 / UNIT))
            wx = lagrange((pos_x & (UNIT - 1)).astype(f32) * (1.0 / UNIT))
            for p in range(4):
                fact_y[pl.ds(g * 64 + p, 8, stride=8), :] = wy[p]
                fact_x[pl.ds(g * 64 + p, 8, stride=8), :] = wx[p]
            floors[0, at, :] = pos_y >> 12
            floors[1, at, :] = pos_x >> 12
        return 0

    lax.fori_loop(0, blocks // 32, factors, 0)

    def two_blocks(first):
        prods = []
        for e in (0, 1):
            b = first + e
            lines = []
            for k in range(3):
                lines.append(spread[dep[k, b]])
            uy = (sub + 1) - jnp.broadcast_to(floors[0, pl.ds(b, 1), :], (8, 128))
            ux = (sub + 1) - jnp.broadcast_to(floors[1, pl.ds(b, 1), :], (8, 128))
            at = pl.ds(pl.multiple_of(b * 8, 8), 8)
            gy = rows_at(fact_y[at, :], uy & 7)
            gx = rows_at(fact_x[at, :], ux & 7)
            near = (ux & 8) == 0
            cols = jnp.concatenate([jnp.where(near, gx, zero), jnp.where(near, zero, gx)], 0).astype(bf16)
            sums = jnp.dot(
                jnp.concatenate(lines, 0), jnp.concatenate([cols] * 8, 0), preferred_element_type=f32
            )
            in0, in1 = uy >= 0, uy >= -8
            for t in range(4):
                r0, r1, r2 = (sums[32 * k + 8 * t : 32 * k + 8 * t + 8] for k in range(3))
                prods.append(jnp.where(in0, r0, jnp.where(in1, r1, r2)) * gy)
        for d in (4, 2, 1):
            prods = [folded(prods[i], prods[i + d], d) for i in range(d)]
        return prods[0]

    def some(i, _):
        for q in range(0, STEP, 4):
            b = i * STEP + q
            four = jnp.concatenate([two_blocks(b), two_blocks(b + 2)], 0).astype(bf16)
            out[pl.ds(pl.multiple_of(b * 4, 16), 16), :] = four
        return 0

    return some


def on_device(tracers, winds, tile_owner, departure):
    pieces = lax.axis_size(AXES)
    blocks = tile_owner.shape[0]
    panel = tracers.shape[0]
    edge = blocks // 4 * panel
    lines = tracers.reshape(panel, blocks, 128).transpose(1, 0, 2).reshape(blocks * panel, 128)
    wind_lines = winds.reshape(2, blocks, 128).transpose(1, 0, 2).reshape(blocks * 2, 128)
    dma = pltpu.SemaphoreType.DMA
    out = pl.pallas_call(
        advect,
        out_shape=jax.ShapeDtypeStruct((blocks * panel, 128), bf16),
        in_specs=[pl.BlockSpec(memory_space=pltpu.HBM)] * 4,
        out_specs=pl.BlockSpec(memory_space=pltpu.HBM),
        scratch_shapes=[
            pltpu.VMEM((blocks * 2, 128), f32),
            pltpu.VMEM((blocks // 128, 128), i32),
            pltpu.VMEM((blocks * panel, 128), bf16),
            pltpu.SMEM((3, blocks), i32),
            pltpu.VMEM((edge, 128), bf16),
            pltpu.VMEM((edge, 128), bf16),
            pltpu.VMEM((blocks, 512), bf16),
            pltpu.VMEM((pieces, 8, 128), i32),
            pltpu.VMEM((pieces, 8, 128), i32),
            pltpu.VMEM((4, 2, 136, 128), i32),
            pltpu.VMEM((8, 128), i32),
            pltpu.VMEM((blocks, 128), i32),
            pltpu.VMEM((blocks * 3 // 2, 32, 128), bf16),
            pltpu.VMEM((blocks * 8, 128), f32),
            pltpu.VMEM((blocks * 8, 128), f32),
            pltpu.VMEM((2, blocks, 128), i32),
            pltpu.VMEM((3, blocks), i32),
            pltpu.VMEM((3, blocks), i32),
            pltpu.VMEM((blocks * panel, 128), bf16),
            dma((3,)),
            dma((pieces,)),
            dma((pieces,)),
            dma((2,)),
            dma((2,)),
            dma((6,)),
            dma((4, 2)),
            dma((5,)),
        ],
        compiler_params=pltpu.CompilerParams(
            collective_id=0, has_side_effects=True, vmem_limit_bytes=60 << 20
        ),
    )(wind_lines, tile_owner.reshape(blocks // 128, 128), lines, departure.T)
    out = pl.pallas_call(
        hand_out,
        out_shape=jax.ShapeDtypeStruct(out.shape, bf16),
        in_specs=[pl.BlockSpec(memory_space=pltpu.HBM)],
        out_specs=pl.BlockSpec(memory_space=pltpu.HBM),
        scratch_shapes=[pltpu.VMEM(out.shape, bf16), dma((4,)), dma((4,))],
        compiler_params=pltpu.CompilerParams(vmem_limit_bytes=60 << 20),
    )(out)
    return out.reshape(blocks, panel, 128).transpose(1, 0, 2).reshape(panel, blocks * 128)


def solution(mesh):
    placed = (
        P("col", AXES),
        P(None, AXES),
        P(AXES),
        P(AXES, None),
    )
    return jax.shard_map(
        on_device, mesh=mesh, in_specs=placed, out_specs=P("col", AXES), check_vma=False
    )
```
